32 devices in a mesh: runs: 2 (over y), slab: 4 (over z), pencil: 2 (over x), sub: 2 (over core).
Axes of the slice: x: 2, y: 2, z: 4, core: 2. Of those that a mesh axis runs over, the one named last changes fastest.
Arguments:
- masses: bfloat16 [262144], P(('runs', 'slab', 'pencil', 'sub')), parts along dimension 0, may hold values from 0.5 to 2
- velocity: float32 [3, 262144], P(None, ('runs', 'slab', 'pencil', 'sub')), parts along dimension 1, may hold values from -6 to 6
- dest_slab: int32 [262144, 1], P(('runs', 'slab', 'pencil', 'sub')), parts along dimension 0, may hold values from 0 to 3; in each aligned block of 8192 rows (0 to 8191, 8192 to 16383, ...) at most 4096 rows name the same one
- dest_cell: int32 [262144], P(('runs', 'slab', 'pencil', 'sub')), parts along dimension 0, may hold values from 0 to 8191
- w_first: bfloat16 [8, 27], replicated, may hold values from -1.25 to 1.25
- w_middle: bfloat16 [8, 216], replicated, may hold values from -0.4375 to 0.4375
- w_last: bfloat16 [3, 216], replicated, may hold values from -0.4375 to 0.4375
- step_size: float32 [1], replicated, may hold values from 0.5 to 2
- cotangent: float32 [3, 262144], P(None, ('runs', 'slab', 'pencil', 'sub')), parts along dimension 1, may hold values from -6 to 6
Outputs:
- velocity_new: float32 [3, 262144], P(None, ('runs', 'slab', 'pencil', 'sub')), parts along dimension 1
- grad_mass: bfloat16 [262144], P(('runs', 'slab', 'pencil', 'sub')), parts along dimension 0
- grad_first: float32 [16, 27], P('runs'), parts along dimension 0
- grad_middle: float32 [16, 216], P('runs'), parts along dimension 0
- grad_last: float32 [6, 216], P('runs'), parts along dimension 0
The draws below stay inside these ranges and needn't reach their ends.
There are 2 independent parts, one for each index of `runs`. The reference program is written for one: setup_inputs(seed, part) draws one part's arguments, and reference() takes and returns one part's arrays. A program takes and returns all parts, laid end to end along the dimension named above; an argument that names none is the same for every part. Nothing has to cross between parts.
Inputs may be any that keep to these rules, and one draw needn't show every extreme that they name: `dest_slab`: among the rows of one device, at most 4096 name the same slab.
All inputs are finite; a program needn't handle non-finite values.
Results may differ from the reference program's by a relative error of at most 0.011.
Values may be sent and summed in bfloat16 or wider, within the bound.
No kernel may reach another device: no remote copies, remote signals or barrier semaphores. Data moves between devices by JAX's collectives and lax.ppermute only.
A program may use at most 64 MiB of HBM per device.

```python
import math
import jax
import jax.numpy as jnp
import numpy as np

ZL = 4
YL = 8
XL = 256
P_DEV = 8192
CH = 8
CELLS_DEV = 8192
SLOTS = 4096
NZ = 16
NY = 32
NCELLS = 131072
PARTICLES = 131072
N_SLAB = 4


def plant(values, rng, smallest, top_value):
    index_at = [jax.random.randint(jax.random.fold_in(rng, axis), (), 0, length) for axis, length in enumerate(values.shape)]
    longest = values.shape.index(max(values.shape))
    next_to = index_at[:longest] + [(index_at[longest] + 1) % values.shape[longest]] + index_at[longest + 1:]
    return values.at[tuple(index_at)].set(smallest).at[tuple(next_to)].set(top_value)


def levels(own_key, dims, cuts, least, high):
    factor_of = 1.0
    for dim, shards_of in cuts:
        steps = jax.random.uniform(jax.random.fold_in(jax.random.fold_in(own_key, 6), dim), (shards_of,), jnp.float32, least / len(cuts), high / len(cuts))
        factor_of = factor_of * jnp.repeat(jnp.exp(steps), dims[dim] // shards_of).reshape((-1,) + (1,) * (len(dims) - 1 - dim))
    return factor_of


def assign_block(stream_key, own, number, rows, amount, top, most, slope):
    order = jax.random.permutation(stream_key, amount)
    crowded, common = load_shares(amount, rows * top, most, slope, True), load_shares(amount, rows * top, most, slope, False)
    places = jnp.arange(amount)

    def named(tallies, rotation):
        used = int((tallies > 0).sum())
        fixed = max(1, used // 4)
        moved = fixed + (places - fixed + rotation * (used - fixed)) % max(1, amount - fixed)
        return jnp.zeros((amount,), jnp.int32).at[order[jnp.where(places < fixed, places, moved)]].set(jnp.asarray(tallies, jnp.int32))

    tallies = jnp.where(number % 4 == 0, named(crowded, number // 4), named(common, number - number // 4 - 1))
    mixed = jax.random.permutation(jax.random.fold_in(own, 3), amount)
    source_of, sink = mixed[0:amount // 2 * 2:2], mixed[1:amount // 2 * 2:2]
    margin = jnp.minimum(tallies[source_of] - 1, most - tallies[sink]) // 2
    margin = jnp.where((source_of == order[0]) | (sink == order[0]) | (tallies[sink] == 0), 0, jnp.maximum(margin, 0))
    moved = jax.random.randint(jax.random.fold_in(own, 4), (amount // 2,), 0, 1 << 20) % (margin + 1)
    tallies = tallies.at[source_of].add(-moved).at[sink].add(moved)
    labels = jnp.searchsorted(jnp.cumsum(tallies), jnp.arange(rows * top), side="right").astype(jnp.int32)
    grid = labels.reshape(top, rows).T
    grid = grid[jax.random.permutation(jax.random.fold_in(own, 1), rows)]
    rotation = jax.random.randint(jax.random.fold_in(own, 2), (rows, 1), 0, top)
    return jnp.take_along_axis(grid, (jnp.arange(top)[None, :] + rotation) % top, axis=1)


def load_shares(count, total, reach, lean, full):
    portions = [(1 << 20) // math.isqrt(standing ** lean) + 1 for standing in range(1, count + 1)]
    largest = reach if full else min(reach, max(-(-total // count), total * portions[0] // sum(portions)))
    least = 1 if total - largest >= count - 1 else 0
    counts, rest = [largest] + [least] * (count - 1), total - largest - least * (count - 1)
    while rest > 0:
        movable = [i for i in range(1, count) if counts[i] < largest] or [i for i in range(1, count) if counts[i] < reach]
        whole, remaining = sum([portions[i] for i in movable]), rest
        for i in movable:
            more = min(reach - counts[i], max(1, remaining * portions[i] // whole), rest)
            counts[i] = counts[i] + more
            rest = rest - more
    return np.array(counts)


def gaussian(key, extent, scale, reach, shards=(), held_as=jnp.bfloat16):
    entries = jax.random.normal(key, extent, jnp.float32) * scale
    if len(shards) > 0:
        entries = levels(key, extent, shards, -0.22, 0.18) * entries
    return jnp.clip(entries, min=-reach, max=reach).astype(held_as)


def setup_inputs(seed: int = 0, part: int = 0) -> dict:
    key_list = jax.random.split(jax.random.key(seed), 10)
    part_keys = jax.random.split(jax.random.fold_in(key_list[9], part), 10)
    masses = jnp.clip(jnp.exp(math.log(2.0) - 1.3862944 * jax.random.uniform(part_keys[0], (PARTICLES,), jnp.float32) ** levels(part_keys[0], (PARTICLES,), ((0, 16),), -0.2, 0.2)), 0.5, 2.0).astype(jnp.bfloat16)
    velocity = gaussian(part_keys[1], (3, PARTICLES), 1.0, 6.0, ((1, 16),), jnp.float32)
    dest_slab_keys = jax.random.split(jax.random.fold_in(part_keys[2], 1), PARTICLES // P_DEV)
    dest_slab_turns = jax.random.permutation(jax.random.fold_in(part_keys[2], 3), PARTICLES // P_DEV)
    dest_slab = jax.vmap(lambda own, number: assign_block(jax.random.fold_in(part_keys[2], 2), own, number, P_DEV, N_SLAB, 1, SLOTS, 2))(dest_slab_keys, dest_slab_turns).reshape((PARTICLES, 1))
    dest_cell = plant(jax.random.randint(part_keys[3], (PARTICLES,), 0, CELLS_DEV), jax.random.fold_in(part_keys[3], 1), 0, CELLS_DEV - 1).astype(jnp.int32)
    w_first = gaussian(key_list[4], (CH, 27), 27 ** -0.5, 1.25)
    w_middle = gaussian(key_list[5], (CH, 27 * CH), (27 * CH) ** -0.5, 0.4375)
    w_last = gaussian(key_list[6], (3, 27 * CH), (27 * CH) ** -0.5, 0.4375)
    step_size = jnp.clip(jnp.exp(jax.random.uniform(key_list[7], (1,), jnp.float32, math.log(0.5), math.log(2.0))), 0.5, 2.0)
    cotangent = gaussian(part_keys[8], (3, PARTICLES), 1.0, 6.0, ((1, 16),), jnp.float32)
    return {"masses": masses, "velocity": velocity, "dest_slab": dest_slab, "dest_cell": dest_cell, "w_first": w_first, "w_middle": w_middle, "w_last": w_last, "step_size": step_size, "cotangent": cotangent}


def offsets():
    listed = []
    for shift_z in (-1, 0, 1):
        for shift_y in (-1, 0, 1):
            for shift_x in (-1, 0, 1):
                listed.append((shift_z, shift_y, shift_x))
    return listed


def silu_slope(pre):
    sigma = jax.nn.sigmoid(pre)
    return sigma * (1.0 + pre * (1.0 - sigma))


def conv_full(field, weight):
    in_channels = field.shape[0]
    result = jnp.zeros((weight.shape[0], field.shape[1] * field.shape[2] * field.shape[3]), jnp.float32)
    for offset_index, offset in enumerate(offsets()):
        shifted = jnp.roll(field, (-offset[0], -offset[1], -offset[2]), axis=(1, 2, 3)).reshape(in_channels, -1)
        weight_cols = weight[:, offset_index * in_channels:(offset_index + 1) * in_channels]
        result = result + jnp.dot(weight_cols, shifted, preferred_element_type=jnp.float32)
    return result


def conv_back_full(grad, weight):
    out_channels = grad.shape[0]
    in_channels = weight.shape[1] // 27
    result = jnp.zeros((in_channels, grad.shape[1] * grad.shape[2] * grad.shape[3]), jnp.float32)
    for offset_index, offset in enumerate(offsets()):
        shifted = jnp.roll(grad, (offset[0], offset[1], offset[2]), axis=(1, 2, 3)).reshape(out_channels, -1)
        weight_cols = weight[:, offset_index * in_channels:(offset_index + 1) * in_channels]
        result = result + jnp.dot(weight_cols.T, shifted, preferred_element_type=jnp.float32)
    return result


def corr_full(delta, field):
    in_channels = field.shape[0]
    pieces = []
    for offset in offsets():
        shifted = jnp.roll(field, (-offset[0], -offset[1], -offset[2]), axis=(1, 2, 3)).reshape(in_channels, -1)
        pieces.append(jnp.dot(delta, shifted.T, preferred_element_type=jnp.float32))
    return jnp.concatenate(pieces, axis=1)


def reference(masses, velocity, dest_slab, dest_cell, w_first, w_middle, w_last, step_size, cotangent):
    holder = jnp.arange(PARTICLES, dtype=jnp.int32) // P_DEV
    column = holder % (NY // YL)
    cell_z = dest_slab[:, 0] * ZL + dest_cell // (YL * XL)
    cell_y = column * YL + (dest_cell // XL) % YL
    cell_x = dest_cell % XL
    global_cell = ((cell_z * NY + cell_y) * XL + cell_x).astype(jnp.int32)
    channels = w_first.shape[0]
    density = jax.ops.segment_sum(masses.astype(jnp.float32), global_cell, num_segments=NCELLS)
    density = density.astype(jnp.bfloat16).reshape(1, NZ, NY, XL)
    pre_one = conv_full(density, w_first)
    act_one = jax.nn.silu(pre_one).astype(jnp.bfloat16).reshape(channels, NZ, NY, XL)
    pre_two = conv_full(act_one, w_middle)
    act_two = jax.nn.silu(pre_two).astype(jnp.bfloat16).reshape(channels, NZ, NY, XL)
    force_mesh = conv_full(act_two, w_last).astype(jnp.bfloat16)
    velocity_new = velocity + step_size[0] * force_mesh[:, global_cell].astype(jnp.float32)
    pushed = (step_size[0] * cotangent).astype(jnp.bfloat16)
    grad_force = jax.ops.segment_sum(pushed.astype(jnp.float32).T, global_cell, num_segments=NCELLS).T
    grad_force = grad_force.astype(jnp.bfloat16)
    scale = NCELLS ** -0.5
    grad_last = corr_full(grad_force, act_two) * scale
    delta_two = (conv_back_full(grad_force.reshape(3, NZ, NY, XL), w_last) * silu_slope(pre_two)).astype(jnp.bfloat16)
    grad_middle = corr_full(delta_two, act_one) * scale
    delta_one = (conv_back_full(delta_two.reshape(channels, NZ, NY, XL), w_middle) * silu_slope(pre_one)).astype(jnp.bfloat16)
    grad_first = corr_full(delta_one, density) * scale
    density_grad = conv_back_full(delta_one.reshape(channels, NZ, NY, XL), w_first).astype(jnp.bfloat16)
    grad_mass = density_grad[0, global_cell]
    return (velocity_new, grad_mass, grad_first, grad_middle, grad_last)
```

```python
import functools
import math

import jax
import jax.numpy as jnp
import numpy as np
from jax import lax
from jax.experimental import pallas as pl
from jax.experimental.pallas import tpu as pltpu
from jax.sharding import PartitionSpec as P

ZL = 4
YL = 8
XL = 256
ROWS = ZL * YL
FIELDS = 4
BLOCK = FIELDS * ROWS
POS = 16
DEPTH = 3 * ZL
BF16 = jnp.bfloat16
F32 = jnp.float32
NT = (((1,), (1,)), ((), ()))
VMEM_LIMIT = 56 * 1024 * 1024


def dot(a, b):
    return jnp.dot(a, b, preferred_element_type=F32)


def dot_nt(a, b):
    return lax.dot_general(a, b, NT, preferred_element_type=F32)


def row_iota(shape, dim):
    return lax.broadcasted_iota(jnp.int32, shape, dim)


def paint_kernel(slabs, step_ref, mass_ref, slab_ref, cell_ref, cot_ref, *rest):
    outs, (hot, lane_hot, total) = rest[:slabs], rest[slabs:]
    turn = pl.program_id(0)
    chunk = mass_ref.shape[1]
    me = lax.axis_index("slab")
    cell = cell_ref[...]
    relative = slab_ref[...] - me
    relative = jnp.where(relative < 0, relative + slabs, relative)
    z, y = cell >> 11, (cell >> 8) & 7
    code = ((relative * 2 + (y >> 2)) << 4) + (z << 2) + (y & 3)

    def tile(row):
        return jnp.broadcast_to(row.astype(F32), (16, chunk)).astype(BF16)

    sixteen = row_iota((16, chunk), 0)
    zero = jnp.zeros((16, chunk), BF16)
    one = jnp.ones((16, chunk), BF16)
    lane = tile(cell & (XL - 1))
    for group in range(XL // 16):
        same = lane == (sixteen + 16 * group).astype(F32).astype(BF16)
        lane_hot[16 * group : 16 * group + 16, :] = jnp.where(same, one, zero)
    values = [tile(mass_ref[...])]
    for component in range(3):
        pushed = (step_ref[0] * cot_ref[component : component + 1, :]).astype(BF16)
        values.append(tile(pushed))
    for base in range(0, 2 * slabs, 16):
        local_code = jnp.clip(code - 16 * base, -1, 256)
        code_tile = tile(local_code)
        for group in range(base, min(base + 16, 2 * slabs)):
            same = code_tile == (sixteen + 16 * (group - base)).astype(F32).astype(BF16)
            for field in range(FIELDS):
                first = group * 64 + field * 16
                hot[first : first + 16, :] = jnp.where(same, values[field], zero)
    part = dot_nt(hot[...], lane_hot[...])

    @pl.when(turn == 0)
    def first_turn():
        total[...] = part

    @pl.when(turn > 0)
    def later_turn():
        total[...] += part

    @pl.when(turn == pl.num_programs(0) - 1)
    def last_turn():
        for k in range(slabs):
            outs[k][...] = total[k * BLOCK : (k + 1) * BLOCK, :].astype(outs[k].dtype)


def paint(step_size, masses, target, cells, cotangent, slabs):
    count = masses.shape[1]
    chunk = math.gcd(count, 2048)
    row = pl.BlockSpec((1, chunk), lambda i: (0, i))
    whole = pl.BlockSpec((BLOCK, XL), lambda i: (0, 0))
    return pl.pallas_call(
        functools.partial(paint_kernel, slabs),
        grid=(count // chunk,),
        in_specs=[
            pl.BlockSpec(memory_space=pltpu.SMEM),
            row,
            row,
            row,
            pl.BlockSpec((3, chunk), lambda i: (0, i)),
        ],
        out_specs=[whole] * slabs,
        out_shape=[
            jax.ShapeDtypeStruct((BLOCK, XL), F32 if k == 0 else BF16) for k in range(slabs)
        ],
        scratch_shapes=[
            pltpu.VMEM((slabs * BLOCK, chunk), BF16),
            pltpu.VMEM((XL, chunk), BF16),
            pltpu.VMEM((slabs * BLOCK, XL), F32),
        ],
        compiler_params=pltpu.CompilerParams(vmem_limit_bytes=VMEM_LIMIT),
    )(step_size, masses, target, cells, cotangent)


def tap_columns(channels):
    width = 9 * channels * POS
    col = np.arange(width)
    pair, channel = col // (channels * POS), (col // POS) % channels
    rows = [((pair // 3 * 3 + b) * 3 + pair % 3) * channels + channel for b in range(3)]
    return np.stack(rows + [np.full(width, -1)] * 5).astype(np.int32)


def tap_hot(taps, b, count):
    width = taps.shape[1]
    same = row_iota((count, width), 0) == taps[b : b + 1, :]
    return jnp.where(same, 1.0, 0.0).astype(F32)


def y_distance(rows, width):
    return (row_iota((rows, width), 1) - row_iota((rows, width), 0)) & (POS - 1)


Y_SHIFTS = (POS - 1, 0, 1)


def band(weight, taps):
    outs, count = weight.shape
    rows, width = outs * POS, taps.shape[1]
    pick = jnp.where(row_iota((rows, outs), 0) >> 4 == row_iota((rows, outs), 1), 1.0, 0.0)
    spread = dot(pick.astype(BF16), weight).astype(BF16)
    distance = y_distance(rows, width)
    result = jnp.zeros((rows, width), F32)
    for b in range(3):
        picked = dot(spread, tap_hot(taps, b, count).astype(BF16))
        result = jnp.where(distance == Y_SHIFTS[b], picked, result)
    return result


def band_kernel(
    first_ref, middle_ref, last_ref, one_ref, many_ref, b1_ref, b2_ref, b3_ref, t1_ref, t2_ref, t3_ref
):
    many = many_ref[...]
    for weight_ref, taps, b_ref, t_ref in (
        (first_ref, one_ref[...], b1_ref, t1_ref),
        (middle_ref, many, b2_ref, t2_ref),
        (last_ref, many, b3_ref, t3_ref),
    ):
        full = band(weight_ref[...], taps)
        b_ref[...] = full.astype(BF16)
        outs, ins = full.shape[0], full.shape[1] // 9
        for pair in range(9):
            block = full[:, pair * ins : (pair + 1) * ins].T.astype(BF16)
            t_ref[:, (8 - pair) * outs : (9 - pair) * outs] = block


def bands(w_first, w_middle, w_last):
    sizes = [(w.shape[0] * POS, w.shape[1] // 27 * POS) for w in (w_first, w_middle, w_last)]
    shapes = [(o, 9 * c) for o, c in sizes] + [(c, 9 * o) for o, c in sizes]
    one = tap_columns(1)
    many = tap_columns(w_middle.shape[1] // 27)
    return pl.pallas_call(
        band_kernel,
        out_shape=[jax.ShapeDtypeStruct(s, BF16) for s in shapes],
        compiler_params=pltpu.CompilerParams(vmem_limit_bytes=VMEM_LIMIT),
        cost_estimate=pl.CostEstimate(
            flops=800_000_000, bytes_accessed=4_000_000, transcendentals=0
        ),
    )(w_first, w_middle, w_last, jnp.asarray(one), jnp.asarray(many))


def lay_out(store, plane, value):
    rows = value.shape[0]
    for e, shift in enumerate((1, 0, XL - 1)):
        moved = value if shift == 0 else pltpu.roll(value, shift, 1)
        store[plane, e * rows : (e + 1) * rows, :] = moved.astype(BF16)


def window(store, plane):
    rows = store.shape[1]
    return store[plane - 1 : plane + 2].reshape(3 * rows, XL)


def centre(store, plane):
    rows = store.shape[1] // 3
    return store[plane, rows : 2 * rows, :]


def slope(pre, sigma):
    return sigma * (1.0 + pre * (1.0 - sigma))


def split_three(value):
    high = value.astype(BF16).astype(F32)
    rest = value - high
    mid = rest.astype(BF16).astype(F32)
    return jnp.concatenate([high, mid, rest - mid], axis=0).astype(BF16)


def weight_sum(full, taps, count):
    outs, width = full.shape[0] // POS, full.shape[1]
    distance = y_distance(YL, width)
    result = None
    for b in range(3):
        rows = [
            jnp.sum(
                jnp.where(distance == Y_SHIFTS[b], full[o * POS : o * POS + YL, :], 0.0),
                axis=0,
                keepdims=True,
            )
            for o in range(outs)
        ]
        rows += [jnp.zeros_like(rows[0])] * (8 - outs)
        parts = dot_nt(split_three(jnp.concatenate(rows, axis=0)), tap_hot(taps, b, count).astype(BF16))
        term = parts[0:8] + parts[8:16] + parts[16:24]
        result = term if result is None else result + term
    return result


def net_kernel(
    below_ref, own_ref, above_ref, before_ref, after_ref,
    b1_ref, b2_ref, b3_ref, t1_ref, t2_ref, t3_ref, one_ref, many_ref, order_ref,
    mesh_ref, grads_ref,
    s0, s1, s2, sg, d2, d1, slope1, slope2, fields,
):
    order = order_ref[...]
    for b, block in enumerate((below_ref, own_ref, above_ref)):
        for c in range(FIELDS):
            pieces = [
                block[c * 16 : c * 16 + 16, :],
                block[64 + c * 16 : 80 + c * 16, :],
                after_ref[b * 64 + c * 16 : b * 64 + c * 16 + 16, :],
                before_ref[b * 64 + c * 16 : b * 64 + c * 16 + 16, :],
            ]
            rows = dot(order, jnp.concatenate(pieces, axis=0))
            for z in range(ZL):
                value = rows[z * POS : (z + 1) * POS, :]
                for e, shift in enumerate((1, 0, XL - 1)):
                    moved = value if shift == 0 else pltpu.roll(value, shift, 1)
                    if c == 0:
                        s0[b * ZL + z, e * 16 : e * 16 + 16, :] = moved.astype(BF16)
                    else:
                        first = e * 48 + (c - 1) * 16
                        sg[b * ZL + z, first : first + 16, :] = moved.astype(BF16)
    b1, b2, b3 = b1_ref[...], b2_ref[...], b3_ref[...]
    t1, t2, t3 = t1_ref[...], t2_ref[...], t3_ref[...]
    for plane in range(1, DEPTH - 1):
        pre = dot(b1, window(s0, plane))
        sigma = jax.nn.sigmoid(pre)
        lay_out(s1, plane, pre * sigma)
        if 3 <= plane < DEPTH - 3:
            slope1[plane] = slope(pre, sigma)
    for plane in range(2, DEPTH - 2):
        pre = dot(b2, window(s1, plane))
        sigma = jax.nn.sigmoid(pre)
        if 3 <= plane < DEPTH - 3:
            lay_out(s2, plane, pre * sigma)
        slope2[plane] = slope(pre, sigma)
    for z in range(ZL):
        force = dot(b3, window(s2, ZL + z))
        for c in range(3):
            first = c * ROWS + z * YL
            fields[first : first + YL, :] = force[c * POS : c * POS + YL, :]
    for plane in range(2, DEPTH - 2):
        lay_out(d2, plane, dot(t3, window(sg, plane)) * slope2[plane])
    for plane in range(3, DEPTH - 3):
        lay_out(d1, plane, dot(t2, window(d2, plane)) * slope1[plane])
    for z in range(ZL):
        pull = dot(t1, window(d1, ZL + z))
        first = 3 * ROWS + z * YL
        fields[first : first + YL, :] = pull[0:YL, :]
    mesh_ref[...] = fields[...].astype(BF16)
    one, many = one_ref[...], many_ref[...]
    grads_ref[...] = jnp.zeros_like(grads_ref)
    for first, (delta, source, taps) in zip(
        (0, 8, 16), ((d1, s0, one), (d2, s1, many), (sg, s2, many))
    ):
        full = None
        for z in range(ZL):
            term = dot_nt(centre(delta, ZL + z), window(source, ZL + z))
            full = term if full is None else full + term
        count = 3 * taps.shape[1] // POS
        grads_ref[first : first + 8, 0:count] = weight_sum(full, taps, count)


def network(blocks, halves, band_list, channels):
    rows = channels * POS
    order = np.zeros((64, 64), np.float32)
    for z in range(4):
        for h in range(4):
            for y in range(4):
                order[z * 16 + h * 4 + y, h * 16 + z * 4 + y] = 1.0
    one, many = tap_columns(1), tap_columns(channels)
    return pl.pallas_call(
        net_kernel,
        out_shape=[
            jax.ShapeDtypeStruct((BLOCK, XL), BF16),
            jax.ShapeDtypeStruct((24, 256), F32),
        ],
        scratch_shapes=[
            pltpu.VMEM((DEPTH, 3 * POS, XL), BF16),
            pltpu.VMEM((DEPTH, 3 * rows, XL), BF16),
            pltpu.VMEM((DEPTH, 3 * rows, XL), BF16),
            pltpu.VMEM((DEPTH, 9 * POS, XL), BF16),
            pltpu.VMEM((DEPTH, 3 * rows, XL), BF16),
            pltpu.VMEM((DEPTH, 3 * rows, XL), BF16),
            pltpu.VMEM((DEPTH, rows, XL), F32),
            pltpu.VMEM((DEPTH, rows, XL), F32),
            pltpu.VMEM((BLOCK, XL), F32),
        ],
        compiler_params=pltpu.CompilerParams(vmem_limit_bytes=VMEM_LIMIT),
    )(*blocks, *halves, *band_list, jnp.asarray(one), jnp.asarray(many), jnp.asarray(order, BF16))


def readout_kernel(slabs, step_ref, slab_ref, cell_ref, velocity_ref, *rest):
    meshes, (velocity_out, mass_out, lane_hot) = rest[:slabs], rest[slabs:]
    chunk = cell_ref.shape[1]
    me = lax.axis_index("slab")
    cell = cell_ref[...]
    relative = slab_ref[...] - me
    relative = jnp.where(relative < 0, relative + slabs, relative)
    code = relative * ROWS + (cell >> 8)
    sixteen = row_iota((16, chunk), 0)
    zero = jnp.zeros((16, chunk), BF16)
    one = jnp.ones((16, chunk), BF16)
    lane = jnp.broadcast_to((cell & (XL - 1)).astype(F32), (16, chunk)).astype(BF16)
    for group in range(XL // 16):
        same = lane == (sixteen + 16 * group).astype(F32).astype(BF16)
        lane_hot[16 * group : 16 * group + 16, :] = jnp.where(same, one, zero)
    code_tile = jnp.broadcast_to(code, (8, chunk))
    eight = row_iota((8, chunk), 0)
    sums = [jnp.zeros((8, chunk), F32) for _ in range(FIELDS)]
    for k in range(slabs):
        rows = dot(meshes[k][...], lane_hot[...])
        for group in range(ROWS // 8):
            same = code_tile == eight + (k * ROWS + group * 8)
            for c in range(FIELDS):
                first = c * ROWS + group * 8
                sums[c] = sums[c] + jnp.where(same, rows[first : first + 8, :], 0.0)
    for c in range(3):
        force = jnp.sum(sums[c], axis=0, keepdims=True)
        velocity_out[c : c + 1, :] = velocity_ref[c : c + 1, :] + step_ref[0] * force
    mass_out[...] = jnp.sum(sums[3], axis=0, keepdims=True).astype(mass_out.dtype)


def read_out(step_size, target, cells, velocity, meshes, slabs):
    count = cells.shape[1]
    chunk = math.gcd(count, 1024)
    row = pl.BlockSpec((1, chunk), lambda i: (0, i))
    three = pl.BlockSpec((3, chunk), lambda i: (0, i))
    whole = pl.BlockSpec((BLOCK, XL), lambda i: (0, 0))
    return pl.pallas_call(
        functools.partial(readout_kernel, slabs),
        grid=(count // chunk,),
        in_specs=[pl.BlockSpec(memory_space=pltpu.SMEM), row, row, three] + [whole] * slabs,
        out_specs=[three, row],
        out_shape=[
            jax.ShapeDtypeStruct((3, count), F32),
            jax.ShapeDtypeStruct((1, count), BF16),
        ],
        scratch_shapes=[pltpu.VMEM((XL, chunk), BF16)],
        compiler_params=pltpu.CompilerParams(vmem_limit_bytes=VMEM_LIMIT),
    )(step_size, target, cells, velocity, *meshes)


def shifted(value, axis, distance):
    count = lax.axis_size(axis)
    return lax.ppermute(value, axis, [(i, (i + distance) % count) for i in range(count)])


def sum_over(value, axis):
    count = lax.axis_size(axis)
    others = [shifted(value, axis, k) for k in range(1, count)]
    return functools.reduce(jnp.add, others, value)


def local(masses, velocity, dest_slab, dest_cell, w_first, w_middle, w_last, step_size, cotangent):
    slabs = lax.axis_size("slab")
    column = ("pencil", "sub")
    count = masses.shape[0]
    target = dest_slab.reshape(1, count)
    cells = dest_cell.reshape(1, count)
    band_list = bands(w_first, w_middle, w_last)
    parts = paint(step_size, masses.reshape(1, count), target, cells, cotangent, slabs)
    arrived = [shifted(parts[k], "slab", k) for k in range(1, slabs)]
    own = functools.reduce(jnp.add, [a.astype(F32) for a in arrived], parts[0]).astype(BF16)
    blocks = (shifted(own, "slab", 1), own, shifted(own, "slab", -1))
    half = BLOCK // 2
    before = shifted(jnp.concatenate([b[half:] for b in blocks], axis=0), column, 1)
    after = shifted(jnp.concatenate([b[:half] for b in blocks], axis=0), column, -1)
    mesh_own, grads = network(blocks, (before, after), band_list, w_middle.shape[0])
    meshes = [mesh_own] + [shifted(mesh_own, "slab", -k) for k in range(1, slabs)]
    grads = sum_over(sum_over(grads, column), "slab")
    velocity_new, grad_mass = read_out(step_size, target, cells, velocity, meshes, slabs)
    cell_total = ZL * YL * XL * slabs * lax.axis_size("pencil") * lax.axis_size("sub")
    grads = grads * (1.0 / math.sqrt(cell_total))
    return (
        velocity_new,
        grad_mass.reshape(count),
        grads[0 : w_first.shape[0], 0 : w_first.shape[1]],
        grads[8 : 8 + w_middle.shape[0], 0 : w_middle.shape[1]],
        grads[16 : 16 + w_last.shape[0], 0 : w_last.shape[1]],
    )


def solution(mesh):
    everywhere = ("runs", "slab", "pencil", "sub")
    placed = (
        P(everywhere),
        P(None, everywhere),
        P(everywhere, None),
        P(everywhere),
        P(),
        P(),
        P(),
        P(),
        P(None, everywhere),
    )
    return jax.shard_map(
        local,
        mesh=mesh,
        in_specs=placed,
        out_specs=(
            P(None, everywhere),
            P(everywhere),
            P("runs", None),
            P("runs", None),
            P("runs", None),
        ),
        check_vma=False,
    )
```

```python
import functools
import math

import jax
import jax.numpy as jnp
import numpy as np
from jax import lax
from jax.experimental import pallas as pl
from jax.experimental.pallas import tpu as pltpu
from jax.sharding import PartitionSpec as P

ZL = 4
YL = 8
XL = 256
ROWS = ZL * YL
FIELDS = 4
BLOCK = FIELDS * ROWS
POS = 16
DEPTH = 3 * ZL
BF16 = jnp.bfloat16
F32 = jnp.float32
NT = (((1,), (1,)), ((), ()))
MIB = 1024 * 1024


def dot(a, b):
    return jnp.dot(a, b, preferred_element_type=F32)


def dot_nt(a, b):
    return lax.dot_general(a, b, NT, preferred_element_type=F32)


def row_iota(shape, dim):
    return lax.broadcasted_iota(jnp.int32, shape, dim)


def spread_rows(dense, height, first, count):
    tiles = [
        jnp.broadcast_to(dense[t : t + 1, :], (height, 128)) for t in range(first, first + count)
    ]
    return jnp.concatenate(tiles, axis=1)


def fill_lane_hot(store, lane, chunk):
    sixteen = row_iota((16, chunk), 0)
    zero, one = jnp.zeros((16, chunk), BF16), jnp.ones((16, chunk), BF16)
    for group in range(XL // 16):
        same = lane == (sixteen + 16 * group).astype(F32).astype(BF16)
        store[16 * group : 16 * group + 16, :] = jnp.where(same, one, zero)


def from_here(target, slabs):
    relative = target - lax.axis_index("slab")
    return jnp.where(relative < 0, relative + slabs, relative)


def paint_kernel(slabs, chunk, step_ref, mass_ref, slab_ref, cell_ref, cot_ref, *rest):
    outs, (hot, lane_hot, total) = rest[:slabs], rest[slabs:]
    cell = cell_ref[...]
    z, y = cell >> 11, (cell >> 8) & 7
    code = ((from_here(slab_ref[...], slabs) * 2 + (y >> 2)) << 4) + (z << 2) + (y & 3)
    lanes = (cell & (XL - 1)).astype(F32)
    mass = mass_ref[...].astype(F32)
    tiles = chunk // 128
    sixteen = row_iota((16, chunk), 0)
    zero = jnp.zeros((16, chunk), BF16)
    bases = range(0, 2 * slabs, 16)
    codes = [jnp.clip(code - 16 * base, -1, 256).astype(F32) for base in bases]
    for turn in range(mass.shape[0] // tiles):
        first_tile = turn * tiles
        here, here_lane = hot.at[turn % 2], lane_hot.at[turn % 2]
        fill_lane_hot(here_lane, spread_rows(lanes, 16, first_tile, tiles).astype(BF16), chunk)
        values = [spread_rows(mass, 16, first_tile, tiles).astype(BF16)]
        for component in range(3):
            pushed = step_ref[0] * cot_ref[component : component + 1, turn * chunk : (turn + 1) * chunk]
            values.append(jnp.broadcast_to(pushed, (16, chunk)).astype(BF16))
        for base, code_part in zip(bases, codes):
            code_tile = spread_rows(code_part, 16, first_tile, tiles).astype(BF16)
            for group in range(base, min(base + 16, 2 * slabs)):
                same = code_tile == (sixteen + 16 * (group - base)).astype(F32).astype(BF16)
                for field in range(FIELDS):
                    first = group * 64 + field * 16
                    here[first : first + 16, :] = jnp.where(same, values[field], zero)
        part = dot_nt(here[...], here_lane[...])
        if turn == 0:
            total[...] = part
        else:
            total[...] += part
    for k in range(slabs):
        outs[k][...] = total[k * BLOCK : (k + 1) * BLOCK, :].astype(outs[k].dtype)


def paint(step_size, masses, target, cells, cotangent, slabs):
    count = cotangent.shape[1]
    chunk = math.gcd(count, 2048)
    scratch = 2 * chunk * (slabs * BLOCK + XL) * 2 + slabs * BLOCK * XL * 4
    vmem = pl.BlockSpec(memory_space=pltpu.VMEM)
    return pl.pallas_call(
        functools.partial(paint_kernel, slabs, chunk),
        in_specs=[pl.BlockSpec(memory_space=pltpu.SMEM)] + [vmem] * 4,
        out_specs=[vmem] * slabs,
        out_shape=[
            jax.ShapeDtypeStruct((BLOCK, XL), F32 if k == 0 else BF16) for k in range(slabs)
        ],
        scratch_shapes=[
            pltpu.VMEM((2, slabs * BLOCK, chunk), BF16),
            pltpu.VMEM((2, XL, chunk), BF16),
            pltpu.VMEM((slabs * BLOCK, XL), F32),
        ],
        compiler_params=pltpu.CompilerParams(vmem_limit_bytes=scratch + 12 * MIB),
    )(step_size, masses, target, cells, cotangent)


def tap_columns(channels):
    width = 9 * channels * POS
    col = np.arange(width)
    pair, channel = col // (channels * POS), (col // POS) % channels
    rows = [((pair // 3 * 3 + b) * 3 + pair % 3) * channels + channel for b in range(3)]
    return np.stack(rows + [np.full(width, -1)] * 5).astype(np.int32)


def tap_hot(taps, b, count):
    width = taps.shape[1]
    same = row_iota((count, width), 0) == taps[b : b + 1, :]
    return jnp.where(same, 1.0, 0.0).astype(F32)


def y_distance(rows, width):
    return (row_iota((rows, width), 1) - row_iota((rows, width), 0)) & (POS - 1)


Y_SHIFTS = (POS - 1, 0, 1)


def band(weight, taps):
    outs, count = weight.shape
    rows, width = outs * POS, taps.shape[1]
    pick = jnp.where(row_iota((rows, outs), 0) >> 4 == row_iota((rows, outs), 1), 1.0, 0.0)
    spread = dot(pick.astype(BF16), weight).astype(BF16)
    distance = y_distance(rows, width)
    result = jnp.zeros((rows, width), F32)
    for b in range(3):
        picked = dot(spread, tap_hot(taps, b, count).astype(BF16))
        result = jnp.where(distance == Y_SHIFTS[b], picked, result)
    return result


def band_kernel(
    first_ref, middle_ref, last_ref, one_ref, many_ref, b1_ref, b2_ref, b3_ref, t1_ref, t2_ref, t3_ref
):
    many = many_ref[...]
    for weight_ref, taps, b_ref, t_ref in (
        (first_ref, one_ref[...], b1_ref, t1_ref),
        (middle_ref, many, b2_ref, t2_ref),
        (last_ref, many, b3_ref, t3_ref),
    ):
        full = band(weight_ref[...], taps)
        b_ref[...] = full.astype(BF16)
        outs, ins = full.shape[0], full.shape[1] // 9
        for pair in range(9):
            block = full[:, pair * ins : (pair + 1) * ins].T.astype(BF16)
            t_ref[:, (8 - pair) * outs : (9 - pair) * outs] = block


def bands(w_first, w_middle, w_last):
    sizes = [(w.shape[0] * POS, w.shape[1] // 27 * POS) for w in (w_first, w_middle, w_last)]
    shapes = [(o, 9 * c) for o, c in sizes] + [(c, 9 * o) for o, c in sizes]
    one = tap_columns(1)
    many = tap_columns(w_middle.shape[1] // 27)
    return pl.pallas_call(
        band_kernel,
        out_shape=[jax.ShapeDtypeStruct(s, BF16) for s in shapes],
        compiler_params=pltpu.CompilerParams(vmem_limit_bytes=20 * MIB),
        cost_estimate=pl.CostEstimate(
            flops=800_000_000, bytes_accessed=4_000_000, transcendentals=0
        ),
    )(w_first, w_middle, w_last, jnp.asarray(one), jnp.asarray(many))


def lay_out(store, plane, value):
    rows = value.shape[0]
    for e, shift in enumerate((1, 0, XL - 1)):
        moved = value if shift == 0 else pltpu.roll(value, shift, 1)
        store[plane, e * rows : (e + 1) * rows, :] = moved.astype(BF16)


def window(store, plane):
    rows = store.shape[1]
    return store[plane - 1 : plane + 2].reshape(3 * rows, XL)


def centre(store, plane):
    rows = store.shape[1] // 3
    return store[plane, rows : 2 * rows, :]


def slope(pre, sigma):
    return sigma * (1.0 + pre * (1.0 - sigma))


def split_three(value):
    high = value.astype(BF16).astype(F32)
    rest = value - high
    mid = rest.astype(BF16).astype(F32)
    return jnp.concatenate([high, mid, rest - mid], axis=0).astype(BF16)


def weight_sum(full, outs, channels):
    width = full.shape[1]
    distance = y_distance(YL, width)
    group = row_iota((width // POS, width), 1) >> 4 == row_iota((width // POS, width), 0)
    group = jnp.where(group, 1.0, 0.0).astype(BF16)
    sums = []
    for b in range(3):
        mask = distance == Y_SHIFTS[b]
        rows = [
            jnp.sum(
                jnp.where(mask, full[o * POS : o * POS + YL, :], 0.0), axis=0, keepdims=True
            )
            for o in range(outs)
        ]
        rows += [jnp.zeros_like(rows[0])] * (8 - outs)
        parts = dot_nt(split_three(jnp.concatenate(rows, axis=0)), group)
        sums.append(parts[0:8] + parts[8:16] + parts[16:24])
    span = 3 * channels
    pieces = [sums[b][:, a * span : (a + 1) * span] for a in range(3) for b in range(3)]
    return jnp.concatenate(pieces, axis=1)


def net_kernel(
    below_ref, own_ref, above_ref, before_ref, after_ref,
    b1_ref, b2_ref, b3_ref, t1_ref, t2_ref, t3_ref, order_ref,
    mesh_ref, grads_ref,
    s0, s1, s2, sg, d2, d1, slope1, slope2, fields,
):
    order = order_ref[...]
    for b, block in enumerate((below_ref, own_ref, above_ref)):
        for c in range(FIELDS):
            pieces = [
                block[c * 16 : c * 16 + 16, :],
                block[64 + c * 16 : 80 + c * 16, :],
                after_ref[b * 64 + c * 16 : b * 64 + c * 16 + 16, :],
                before_ref[b * 64 + c * 16 : b * 64 + c * 16 + 16, :],
            ]
            rows = dot(order, jnp.concatenate(pieces, axis=0))
            for z in range(ZL):
                value = rows[z * POS : (z + 1) * POS, :]
                for e, shift in enumerate((1, 0, XL - 1)):
                    moved = value if shift == 0 else pltpu.roll(value, shift, 1)
                    if c == 0:
                        s0[b * ZL + z, e * 16 : e * 16 + 16, :] = moved.astype(BF16)
                    else:
                        first = e * 48 + (c - 1) * 16
                        sg[b * ZL + z, first : first + 16, :] = moved.astype(BF16)
    b1, b2, b3 = b1_ref[...], b2_ref[...], b3_ref[...]
    t1, t2, t3 = t1_ref[...], t2_ref[...], t3_ref[...]
    for plane in range(1, DEPTH - 1):
        pre = dot(b1, window(s0, plane))
        sigma = jax.nn.sigmoid(pre)
        lay_out(s1, plane, pre * sigma)
        if 3 <= plane < DEPTH - 3:
            slope1[plane] = slope(pre, sigma)
    for plane in range(2, DEPTH - 2):
        pre = dot(b2, window(s1, plane))
        sigma = jax.nn.sigmoid(pre)
        if 3 <= plane < DEPTH - 3:
            lay_out(s2, plane, pre * sigma)
        slope2[plane] = slope(pre, sigma)
    for z in range(ZL):
        force = dot(b3, window(s2, ZL + z))
        for c in range(3):
            first = c * ROWS + z * YL
            fields[first : first + YL, :] = force[c * POS : c * POS + YL, :]
    for plane in range(2, DEPTH - 2):
        lay_out(d2, plane, dot(t3, window(sg, plane)) * slope2[plane])
    for plane in range(3, DEPTH - 3):
        lay_out(d1, plane, dot(t2, window(d2, plane)) * slope1[plane])
    for z in range(ZL):
        pull = dot(t1, window(d1, ZL + z))
        first = 3 * ROWS + z * YL
        fields[first : first + YL, :] = pull[0:YL, :]
    mesh_ref[...] = fields[...].astype(BF16)
    grads_ref[...] = jnp.zeros_like(grads_ref)
    channels = s1.shape[1] // (3 * POS)
    for first, (delta, source, outs, ins) in zip(
        (0, 8, 16), ((d1, s0, channels, 1), (d2, s1, channels, channels), (sg, s2, 3, channels))
    ):
        full = None
        for z in range(ZL):
            term = dot_nt(centre(delta, ZL + z), window(source, ZL + z))
            full = term if full is None else full + term
        grads_ref[first : first + 8, 0 : 27 * ins] = weight_sum(full, outs, ins)


def network(blocks, halves, band_list, channels):
    rows = channels * POS
    order = np.zeros((64, 64), np.float32)
    for z in range(4):
        for h in range(4):
            for y in range(4):
                order[z * 16 + h * 4 + y, h * 16 + z * 4 + y] = 1.0
    return pl.pallas_call(
        net_kernel,
        out_shape=[
            jax.ShapeDtypeStruct((BLOCK, XL), BF16),
            jax.ShapeDtypeStruct((24, 256), F32),
        ],
        scratch_shapes=[
            pltpu.VMEM((DEPTH, 3 * POS, XL), BF16),
            pltpu.VMEM((DEPTH, 3 * rows, XL), BF16),
            pltpu.VMEM((DEPTH, 3 * rows, XL), BF16),
            pltpu.VMEM((DEPTH, 9 * POS, XL), BF16),
            pltpu.VMEM((DEPTH, 3 * rows, XL), BF16),
            pltpu.VMEM((DEPTH, 3 * rows, XL), BF16),
            pltpu.VMEM((DEPTH, rows, XL), F32),
            pltpu.VMEM((DEPTH, rows, XL), F32),
            pltpu.VMEM((BLOCK, XL), F32),
        ],
        compiler_params=pltpu.CompilerParams(vmem_limit_bytes=28 * MIB),
    )(*blocks, *halves, *band_list, jnp.asarray(order, BF16))


def readout_kernel(slabs, chunk, stages, scale, step_ref, slab_ref, cell_ref, velocity_ref, *rest):
    meshes, rest = rest[:slabs], rest[slabs:]
    grads, rest = rest[:stages], rest[stages:]
    velocity_out, mass_out, first_out, middle_out, last_out, lane_hot, mass_rows = rest
    total = grads[0][...]
    for other in grads[1:]:
        total = total + other[...]
    total = total * scale
    first_out[...] = total[0 : first_out.shape[0], 0 : first_out.shape[1]]
    middle_out[...] = total[8 : 8 + middle_out.shape[0], 0 : middle_out.shape[1]]
    last_out[...] = total[16 : 16 + last_out.shape[0], 0 : last_out.shape[1]]
    cell = cell_ref[...]
    code = from_here(slab_ref[...], slabs) * ROWS + (cell >> 8)
    lanes = (cell & (XL - 1)).astype(F32)
    eight = row_iota((8, chunk), 0)
    tiles = chunk // 128
    for turn in range(cell.shape[0] // tiles):
        here = lane_hot.at[turn % 2]
        fill_lane_hot(here, spread_rows(lanes, 16, turn * tiles, tiles).astype(BF16), chunk)
        code_tile = spread_rows(code, 8, turn * tiles, tiles)
        sums = [jnp.zeros((8, chunk), F32) for _ in range(FIELDS)]
        for k in range(slabs):
            rows = dot(meshes[k][...], here[...])
            for group in range(ROWS // 8):
                same = code_tile == eight + (k * ROWS + group * 8)
                for c in range(FIELDS):
                    first = c * ROWS + group * 8
                    sums[c] = sums[c] + jnp.where(same, rows[first : first + 8, :], 0.0)
        span = slice(turn * chunk, (turn + 1) * chunk)
        for c in range(3):
            force = jnp.sum(sums[c], axis=0, keepdims=True)
            velocity_out[c : c + 1, span] = velocity_ref[c : c + 1, span] + step_ref[0] * force
        pull = jnp.sum(sums[3], axis=0, keepdims=True)
        for t in range(tiles):
            mass_rows[turn * tiles + t : turn * tiles + t + 1, :] = pull[:, t * 128 : (t + 1) * 128]
    mass_out[...] = mass_rows[...].astype(BF16)


def read_out(step_size, target, cells, velocity, meshes, grads, weights, scale, slabs):
    count = velocity.shape[1]
    chunk = math.gcd(count, 1024)
    vmem = pl.BlockSpec(memory_space=pltpu.VMEM)
    return pl.pallas_call(
        functools.partial(readout_kernel, slabs, chunk, len(grads), scale),
        in_specs=[pl.BlockSpec(memory_space=pltpu.SMEM)]
        + [vmem] * (3 + len(meshes) + len(grads)),
        out_specs=[vmem] * 5,
        out_shape=[
            jax.ShapeDtypeStruct((3, count), F32),
            jax.ShapeDtypeStruct((count // 128, 128), BF16),
        ]
        + [jax.ShapeDtypeStruct(w.shape, F32) for w in weights],
        scratch_shapes=[
            pltpu.VMEM((2, XL, chunk), BF16),
            pltpu.VMEM((count // 128, 128), F32),
        ],
        compiler_params=pltpu.CompilerParams(vmem_limit_bytes=24 * MIB),
        cost_estimate=pl.CostEstimate(
            flops=slabs * 2 * BLOCK * XL * count, bytes_accessed=1_000_000, transcendentals=0
        ),
    )(step_size, target, cells, velocity, *meshes, *grads)


def shifted(value, axis, distance):
    count = lax.axis_size(axis)
    return lax.ppermute(value, axis, [(i, (i + distance) % count) for i in range(count)])


def from_all(value, axis):
    return [value] + [shifted(value, axis, -k) for k in range(1, lax.axis_size(axis))]


def local(masses, velocity, dest_slab, dest_cell, w_first, w_middle, w_last, step_size, cotangent):
    slabs = lax.axis_size("slab")
    column = ("pencil", "sub")
    count = masses.shape[0]
    dense = (count // 128, 128)
    target, cells = dest_slab.reshape(dense), dest_cell.reshape(dense)
    band_list = bands(w_first, w_middle, w_last)
    parts = paint(step_size, masses.reshape(dense), target, cells, cotangent, slabs)
    arrived = [shifted(parts[k], "slab", k) for k in range(1, slabs)]
    own = functools.reduce(jnp.add, [a.astype(F32) for a in arrived], parts[0]).astype(BF16)
    own, band_list = lax.optimization_barrier((own, band_list))
    blocks = (shifted(own, "slab", 1), own, shifted(own, "slab", -1))
    half = BLOCK // 2
    before = shifted(jnp.concatenate([b[half:] for b in blocks], axis=0), column, 1)
    after = shifted(jnp.concatenate([b[:half] for b in blocks], axis=0), column, -1)
    mesh_own, grads = network(blocks, (before, after), band_list, w_middle.shape[0])
    meshes = from_all(mesh_own, "slab")
    grads = functools.reduce(jnp.add, from_all(grads, column))
    cell_total = ZL * YL * XL * slabs * lax.axis_size("pencil") * lax.axis_size("sub")
    velocity_new, grad_mass, *weight_grads = read_out(
        step_size, target, cells, velocity, meshes, from_all(grads, "slab"),
        (w_first, w_middle, w_last), 1.0 / math.sqrt(cell_total), slabs,
    )
    return (velocity_new, grad_mass.reshape(count), *weight_grads)


def solution(mesh):
    everywhere = ("runs", "slab", "pencil", "sub")
    placed = (
        P(everywhere),
        P(None, everywhere),
        P(everywhere, None),
        P(everywhere),
        P(),
        P(),
        P(),
        P(),
        P(None, everywhere),
    )
    return jax.shard_map(
        local,
        mesh=mesh,
        in_specs=placed,
        out_specs=(
            P(None, everywhere),
            P(everywhere),
            P("runs", None),
            P("runs", None),
            P("runs", None),
        ),
        check_vma=False,
    )
```

```python
import functools
import math

import jax
import jax.numpy as jnp
import numpy as np
from jax import lax
from jax.experimental import pallas as pl
from jax.experimental.pallas import tpu as pltpu
from jax.sharding import PartitionSpec as P

ZL = 4
YL = 8
XL = 256
ROWS = ZL * YL
FIELDS = 4
POS = 16
HALF = POS // 4
BF16 = jnp.bfloat16
F32 = jnp.float32
NT = (((1,), (1,)), ((), ()))
MIB = 1024 * 1024
VMEM = pl.BlockSpec(memory_space=pltpu.VMEM)
SMEM = pl.BlockSpec(memory_space=pltpu.SMEM)


def dot(a, b):
    return jnp.dot(a, b, preferred_element_type=F32)


def dot_nt(a, b):
    return lax.dot_general(a, b, NT, preferred_element_type=F32)


def row_iota(shape, dim):
    return lax.broadcasted_iota(jnp.int32, shape, dim)


def limit(size):
    return pltpu.CompilerParams(vmem_limit_bytes=size)


def pack_kernel(step_ref, mass_ref, slab_ref, cell_ref, cot_ref, out_ref, rows):
    tiles = mass_ref.shape[0]
    cell, slab = cell_ref[...], slab_ref[...]
    z, y = cell >> 11, (cell >> 8) & 7
    code = ((slab & 7) << 5) + ((y >> 2) << 4) + (z << 2) + (y & 3)
    for component in range(3):
        for t in range(tiles):
            row = component * tiles + t
            rows[row : row + 1, :] = cot_ref[component : component + 1, t * 128 : (t + 1) * 128]
    out_ref[0:tiles, :] = mass_ref[...]
    out_ref[tiles : 4 * tiles, :] = (step_ref[0] * rows[...]).astype(BF16)
    out_ref[4 * tiles : 5 * tiles, :] = code.astype(F32).astype(BF16)
    out_ref[5 * tiles : 6 * tiles, :] = (cell & (XL - 1)).astype(F32).astype(BF16)
    if out_ref.shape[0] > 6 * tiles:
        out_ref[6 * tiles : 7 * tiles, :] = (slab >> 3).astype(F32).astype(BF16)


def pack(step_size, masses, target, cells, cotangent, slabs):
    tiles = masses.shape[0]
    return pl.pallas_call(
        pack_kernel,
        in_specs=[SMEM] + [VMEM] * 4,
        out_specs=VMEM,
        out_shape=jax.ShapeDtypeStruct(((6 if slabs <= 8 else 7) * tiles, 128), BF16),
        scratch_shapes=[pltpu.VMEM((3 * tiles, 128), F32)],
        compiler_params=limit(60 * MIB),
    )(step_size, masses, target, cells, cotangent)


def spread_rows(dense, height, first, count):
    tiles = [
        jnp.broadcast_to(dense[t : t + 1, :], (height, 128)) for t in range(first, first + count)
    ]
    return jnp.concatenate(tiles, axis=1)


def fill_lane_hot(store, lane, chunk):
    sixteen = row_iota((16, chunk), 0)
    zero, one = jnp.zeros((16, chunk), BF16), jnp.ones((16, chunk), BF16)
    for group in range(XL // 16):
        same = lane == (sixteen + 16 * group).astype(F32).astype(BF16)
        store[16 * group : 16 * group + 16, :] = jnp.where(same, one, zero)


def paint_kernel(slabs, chunk, tiles, started, final, *refs):
    before, refs = (refs[0], refs[1:]) if started else (None, refs)
    message, refs = refs[0], refs[1:]
    outs, (hot, lane_hot, total) = refs[:-3], refs[-3:]
    step = chunk // 128
    sixteen = row_iota((16, chunk), 0)
    zero = jnp.zeros((16, chunk), BF16)
    for turn in range(tiles // step):
        here, here_lane = hot.at[turn % 2], lane_hot.at[turn % 2]

        def spread(field):
            rows = message[field * tiles : (field + 1) * tiles, :].astype(F32)
            return spread_rows(rows, 16, turn * step, step)

        fill_lane_hot(here_lane, spread(5).astype(BF16), chunk)
        values = [spread(field).astype(BF16) for field in range(FIELDS)]
        code = spread(4)
        for eight in range(0, slabs, 8):
            code_tile = code if slabs <= 8 else jnp.where(spread(6) == eight // 8, code, -1.0)
            code_tile = code_tile.astype(BF16)
            for slab in range(eight, min(eight + 8, slabs)):
                for half in range(2):
                    place = ((slab - eight) * 2 + half) * 16
                    same = code_tile == (sixteen + place).astype(F32).astype(BF16)
                    for field in range(FIELDS):
                        first = ((half * FIELDS + field) * slabs + slab) * 16
                        here[first : first + 16, :] = jnp.where(same, values[field], zero)
        part = dot_nt(here[...], here_lane[...])
        if turn > 0:
            total[...] += part
        elif started:
            total[...] = before[...] + part
        else:
            total[...] = part
    if final:
        middle = total.shape[0] // 2
        outs[0][...] = total[:middle, :].astype(BF16)
        outs[1][...] = total[middle:, :].astype(BF16)
    else:
        outs[0][...] = total[...]


def paint(before, message, tiles, slabs, final):
    chunk = 128 * math.gcd(tiles, 16)
    height = 2 * FIELDS * slabs * 16
    scratch = 2 * chunk * (height + XL) * 2 + height * XL * 4
    shapes = [jax.ShapeDtypeStruct((height, XL), F32)]
    if final:
        shapes = [jax.ShapeDtypeStruct((height // 2, XL), BF16)] * 2
    given = [message] if before is None else [before, message]
    return pl.pallas_call(
        functools.partial(paint_kernel, slabs, chunk, tiles, before is not None, final),
        in_specs=[VMEM] * len(given),
        out_specs=[VMEM] * len(shapes),
        out_shape=shapes,
        scratch_shapes=[
            pltpu.VMEM((2, height, chunk), BF16),
            pltpu.VMEM((2, XL, chunk), BF16),
            pltpu.VMEM((height, XL), F32),
        ],
        compiler_params=limit(scratch + height * XL * 12 + 8 * MIB),
        cost_estimate=pl.CostEstimate(
            flops=2 * height * XL * tiles * 128, bytes_accessed=MIB, transcendentals=0
        ),
    )(*given)


def y_of(place):
    rest = place - 8
    if isinstance(place, np.ndarray):
        return np.where(place < 8, place + 4, np.where(rest % 2 == 0, 12 + rest // 2, 3 - rest // 2))
    halo = jnp.where((rest & 1) == 0, 12 + (rest >> 1), 3 - (rest >> 1))
    return jnp.where(place < 8, place + 4, halo)


def columns(rows, channels):
    col = np.arange(9 * rows * channels)
    pair, place, channel = col // (rows * channels), col // channels % rows, col % channels
    taps = [((pair // 3 * 3 + b) * 3 + pair % 3) * channels + channel for b in range(3)]
    return np.stack(taps + [y_of(place)] + [np.zeros_like(col)] * 4).astype(np.int32)


def window_columns(rows, channels):
    col = np.arange(3 * rows * channels)
    listed = [y_of(col // channels % rows), col // (rows * channels) * channels + col % channels]
    return np.stack(listed + [np.zeros_like(col)] * 6).astype(np.int32)


def band(weight, table, row_channel, row_place):
    outs, count = weight.shape
    width = table.shape[1]
    rows = row_channel.shape[0]
    pick = jnp.where(row_channel[:, 0:outs] == row_iota((rows, outs), 1), 1.0, 0.0)
    spread = dot(pick.astype(BF16), weight).astype(BF16)
    distance = table[3:4, :] - y_of(row_place)
    result = jnp.zeros((rows, width), F32)
    for b in range(3):
        same = row_iota((count, width), 0) == table[b : b + 1, :]
        picked = dot(spread, jnp.where(same, 1.0, 0.0).astype(BF16))
        result = jnp.where(distance == b - 1, picked, result)
    return result


def band_kernel(
    first_ref, middle_ref, last_ref, c1_ref, c2_ref, c3_ref,
    b1_ref, b2_ref, b3_ref, t1_ref, t2_ref, t3_ref,
):
    channels = first_ref.shape[0]
    bits = channels.bit_length() - 1

    def mixed(rows, width):
        row = row_iota((rows, width), 0)
        return row & (channels - 1), row >> bits

    def turned(full, pair, width, rows, out_ref):
        block = full[:, pair * width : (pair + 1) * width].T[0:rows].astype(BF16)
        out_ref[:, (8 - pair) * block.shape[1] : (9 - pair) * block.shape[1]] = block

    def stack(out_ref, pair, block):
        rows, width = block.shape
        first = pair % 3 * width
        out_ref[pair // 3 * rows : (pair // 3 + 1) * rows, first : first + width] = block

    rows = b1_ref.shape[0]
    table = c1_ref[...]
    full = band(first_ref[...], table, mixed(rows, 128)[0], mixed(rows, table.shape[1])[1])
    b1_ref[...] = full.astype(BF16)
    short = t1_ref.shape[1] // 3
    for pair in range(9):
        stack(t1_ref, 8 - pair, full[0:short, pair * POS : (pair + 1) * POS].T.astype(BF16))
    rows = b2_ref.shape[0]
    table = c2_ref[...]
    full = band(middle_ref[...], table, mixed(rows, 128)[0], mixed(rows, table.shape[1])[1])
    b2_ref[...] = full.astype(BF16)
    for pair in range(9):
        turned(full, pair, full.shape[1] // 9, t2_ref.shape[0], t2_ref)
    rows = 3 * POS
    table = c3_ref[...]
    channel = row_iota((rows, 128), 0) >> 4
    full = band(last_ref[...], table, channel, row_iota((rows, table.shape[1]), 0) & (POS - 1))
    width, short = full.shape[1] // 9, b3_ref.shape[1] // 3
    own = [full[o * POS : o * POS + YL] for o in range(3)] + [jnp.zeros((YL, full.shape[1]), F32)]
    own = jnp.concatenate(own, axis=0).astype(BF16)
    for pair in range(9):
        stack(b3_ref, pair, own[:, pair * width : pair * width + short])
        turned(full, pair, width, t3_ref.shape[0], t3_ref)


def bands(w_first, w_middle, w_last):
    c = w_middle.shape[0]
    tables = [jnp.asarray(t) for t in (columns(16, 1), columns(14, c), columns(12, c))]
    shapes = [
        (14 * c, 9 * 16), (12 * c, 9 * 14 * c), (3 * 4 * YL, 3 * 10 * c),
        (3 * POS, 3 * 10 * c), (10 * c, 9 * 12 * c), (12 * c, 9 * 3 * POS),
    ]
    return pl.pallas_call(
        band_kernel,
        in_specs=[VMEM] * 6,
        out_specs=[VMEM] * 6,
        out_shape=[jax.ShapeDtypeStruct(s, BF16) for s in shapes],
        compiler_params=limit(20 * MIB),
        cost_estimate=pl.CostEstimate(
            flops=800_000_000, bytes_accessed=4_000_000, transcendentals=0
        ),
    )(w_first, w_middle, w_last, *tables)


def slope(pre, sigma):
    return sigma * (1.0 + pre * (1.0 - sigma))


def split_three(value):
    high = value.astype(BF16).astype(F32)
    rest = value - high
    mid = rest.astype(BF16).astype(F32)
    return jnp.concatenate([high, mid, rest - mid], axis=0).astype(BF16)


def weight_sum(full, table, channels, mixed, outs):
    count, width = full.shape[0] // 3, full.shape[1]
    group = row_iota((3 * channels, width), 0) == table[1:2, :]
    group = jnp.where(group, 1.0, 0.0).astype(BF16)
    picked = []
    for b in range(3):
        for e in range(3):
            block = full[e * count : (e + 1) * count, :]
            if mixed:
                parts = [
                    jnp.where(table[0:1, :] == place + 3 + b, block[place * 8 : place * 8 + 8, :], 0.0)
                    for place in range(YL)
                ]
                picked.append(functools.reduce(jnp.add, parts))
                continue
            wanted = table[0:1, :] - row_iota((YL, width), 0) == 3 + b
            rows = [
                jnp.sum(
                    jnp.where(wanted, block[o * POS : o * POS + YL, :], 0.0), axis=0, keepdims=True
                )
                for o in range(outs)
            ]
            picked.append(jnp.concatenate(rows + [jnp.zeros_like(rows[0])] * (8 - outs), axis=0))
    parts = dot_nt(split_three(jnp.concatenate(picked, axis=0)), group)
    total = parts[0:72] + parts[72:144] + parts[144:216]
    pieces = [
        total[pair * 8 : pair * 8 + 8, a * channels : (a + 1) * channels]
        for a in range(3)
        for pair in range(9)
    ]
    return jnp.concatenate(pieces, axis=1)


class Store:
    def __init__(self, ref, depth, rows):
        self.ref, self.depth, self.rows = ref, depth, rows

    def put(self, plane, value, first=0):
        places = [plane + 1]
        if plane == 0:
            places.append(self.depth + 1)
        if plane == self.depth - 1:
            places.append(0)
        for e, shift in enumerate((1, 0, XL - 1)):
            moved = (value if shift == 0 else pltpu.roll(value, shift, 1)).astype(BF16)
            for place in places:
                row = (place * 3 + e) * self.rows + first
                self.ref[row : row + value.shape[0], :] = moved

    def window(self, plane):
        return self.ref[plane * 3 * self.rows : (plane + 3) * 3 * self.rows, :]

    def plane(self, plane):
        return self.ref[(plane + 1) * 3 * self.rows : (plane + 2) * 3 * self.rows, :]

    def shifted(self, plane, e, count):
        row = ((plane + 1) * 3 + e) * self.rows
        return self.ref[row : row + count, :]


def products(delta, count, source, depth):
    total = None
    for plane in range(0, depth, 4):
        left, right = [
            jnp.concatenate([rows(plane + k) for k in range(4)], axis=1)
            for rows in (
                lambda p: jnp.concatenate([delta.shifted(p, e, count) for e in (2, 1, 0)], axis=0),
                lambda p: jnp.concatenate(
                    [source.shifted(p + a, 1, source.rows) for a in (-1, 0, 1)], axis=0
                ),
            )
        ]
        if source.rows < count:
            term = dot_nt(left, right)
        else:
            term = dot_nt(right, left)
        total = term if total is None else total + term
    return total if source.rows < count else total.T


def stacked(weight, store, depth):
    rows = weight.shape[0] // 3
    parts = [dot(weight, store.plane(plane)) for plane in range(depth)]
    return [
        parts[(plane - 1) % depth][0:rows]
        + parts[plane][rows : 2 * rows]
        + parts[(plane + 1) % depth][2 * rows :]
        for plane in range(depth)
    ]


def net_kernel(
    slabs, channels, shared,
    low_ref, high_ref, after_ref, before_ref,
    b1_ref, b2_ref, b3_ref, t1_ref, t2_ref, t3_ref, order_ref, c1_ref, c2_ref, c3_ref,
    mesh_ref, grads_ref,
    s0_ref, sg_ref, a_ref, b_ref, slope1, slope2, fields, *more,
):
    depth = slabs * ZL
    s0, sg = Store(s0_ref, depth, POS), Store(sg_ref, depth, 3 * POS)
    s1, s2 = Store(a_ref, depth, 14 * channels), Store(b_ref, depth, 10 * channels)
    d2 = Store(b_ref if shared else more[0], depth, 12 * channels)
    d1 = Store(a_ref if shared else more[1], depth, 10 * channels)
    order = order_ref[...]
    for slab in range(slabs):
        for c in range(FIELDS):
            first = (c * slabs + slab) * 16
            pieces = [ref[first : first + 16, :] for ref in (low_ref, high_ref, after_ref, before_ref)]
            rows = dot(order, jnp.concatenate(pieces, axis=0))
            for z in range(ZL):
                value = rows[z * POS : (z + 1) * POS, :]
                if c == 0:
                    s0.put(slab * ZL + z, value)
                else:
                    sg.put(slab * ZL + z, value, (c - 1) * POS)
    grads_ref[...] = jnp.zeros_like(grads_ref)
    inner, outer = 10 * channels, 12 * channels
    b1 = b1_ref[...]
    for plane in range(depth):
        pre = dot(b1, s0.window(plane))
        sigma = jax.nn.sigmoid(pre)
        s1.put(plane, pre * sigma)
        slope1[plane] = slope(pre[0:inner], sigma[0:inner])
    b2 = b2_ref[...]
    for plane in range(depth):
        pre = dot(b2, s1.window(plane))
        sigma = jax.nn.sigmoid(pre)
        s2.put(plane, pre[0:inner] * sigma[0:inner])
        slope2[plane] = slope(pre, sigma)

    def place(plane, field):
        first = (plane // ZL * FIELDS + field) * ROWS + plane % ZL * YL
        return slice(first, first + YL)

    for plane, force in enumerate(stacked(b3_ref[...], s2, depth)):
        for c in range(3):
            fields[place(plane, c), :] = force[c * YL : (c + 1) * YL, :]
    full = products(sg, 3 * POS, s2, depth)
    grads_ref[16:24, 0 : 27 * channels] = weight_sum(full, c3_ref[...], channels, False, 3)
    t3 = t3_ref[...]
    for plane in range(depth):
        d2.put(plane, dot(t3, sg.window(plane)) * slope2[plane])
    full = products(d2, YL * channels, s1, depth)
    grads_ref[8:16, 0 : 27 * channels] = weight_sum(full, c2_ref[...], channels, True, channels)
    t2 = t2_ref[...]
    for plane in range(depth):
        d1.put(plane, dot(t2, d2.window(plane)) * slope1[plane])
    full = products(d1, YL * channels, s0, depth)
    grads_ref[0:8, 0:27] = weight_sum(full, c1_ref[...], 1, True, channels)
    for plane, pull in enumerate(stacked(t1_ref[...], d1, depth)):
        fields[place(plane, 3), :] = pull[0:YL, :]
    mesh_ref[...] = fields[...].astype(BF16)


def network(halves, band_list, channels, slabs):
    depth = slabs * ZL
    order = np.zeros((64, 64), np.float32)
    for z in range(4):
        for y in range(4):
            for h, place in enumerate((y, 4 + y, 8 + 2 * y, 15 - 2 * y)):
                order[z * 16 + place, h * 16 + z * 4 + y] = 1.0
    planes = 3 * (depth + 2)
    shared = slabs > 4
    sizes = [POS, 3 * POS, 14 * channels, (12 if shared else 10) * channels]
    stores = [pltpu.VMEM((planes * n, XL), BF16) for n in sizes]
    more = [] if shared else [12 * channels, 10 * channels]
    slopes = [pltpu.VMEM((depth, n * channels, XL), F32) for n in (10, 12)]
    size = sum(sizes + more) * planes * XL * 2 + (22 * channels + 32) * depth * XL * 4
    tables = [jnp.asarray(t) for t in (window_columns(16, 1), window_columns(14, channels), window_columns(10, channels))]
    given = (*halves, *band_list, jnp.asarray(order, BF16), *tables)
    return pl.pallas_call(
        functools.partial(net_kernel, slabs, channels, shared),
        in_specs=[VMEM] * len(given),
        out_specs=[VMEM] * 2,
        out_shape=[
            jax.ShapeDtypeStruct((slabs * FIELDS * ROWS, XL), BF16),
            jax.ShapeDtypeStruct((24, 256), F32),
        ],
        scratch_shapes=stores
        + slopes
        + [pltpu.VMEM((slabs * FIELDS * ROWS, XL), F32)]
        + [pltpu.VMEM((planes * n, XL), BF16) for n in more],
        compiler_params=limit(size + 12 * MIB),
    )(*given)


def readout_kernel(slabs, chunk, step_ref, slab_ref, cell_ref, velocity_ref, mesh_ref, *rest):
    velocity_out, mass_out, lane_hot, mass_rows = rest
    cell = cell_ref[...]
    code = slab_ref[...] * ROWS + (cell >> 8)
    lanes = (cell & (XL - 1)).astype(F32)
    eight = row_iota((8, chunk), 0)
    tiles = chunk // 128
    height = FIELDS * ROWS
    for turn in range(cell.shape[0] // tiles):
        here = lane_hot.at[turn % 2]
        fill_lane_hot(here, spread_rows(lanes, 16, turn * tiles, tiles).astype(BF16), chunk)
        code_tile = spread_rows(code, 8, turn * tiles, tiles)
        sums = [jnp.zeros((8, chunk), F32) for _ in range(FIELDS)]
        for k in range(slabs):
            rows = dot(mesh_ref[k * height : (k + 1) * height, :], here[...])
            for group in range(ROWS // 8):
                same = code_tile == eight + (k * ROWS + group * 8)
                for c in range(FIELDS):
                    first = c * ROWS + group * 8
                    sums[c] = sums[c] + jnp.where(same, rows[first : first + 8, :], 0.0)
        span = slice(turn * chunk, (turn + 1) * chunk)
        for c in range(3):
            force = jnp.sum(sums[c], axis=0, keepdims=True)
            velocity_out[c : c + 1, span] = velocity_ref[c : c + 1, span] + step_ref[0] * force
        pull = jnp.sum(sums[3], axis=0, keepdims=True)
        for t in range(tiles):
            mass_rows[turn * tiles + t : turn * tiles + t + 1, :] = pull[:, t * 128 : (t + 1) * 128]
    mass_out[...] = mass_rows[...].astype(BF16)


def read_out(step_size, target, cells, velocity, mesh, slabs):
    count = velocity.shape[1]
    chunk = math.gcd(count, 1024)
    return pl.pallas_call(
        functools.partial(readout_kernel, slabs, chunk),
        in_specs=[SMEM] + [VMEM] * 4,
        out_specs=[VMEM] * 2,
        out_shape=[
            jax.ShapeDtypeStruct((3, count), F32),
            jax.ShapeDtypeStruct((count // 128, 128), BF16),
        ],
        scratch_shapes=[
            pltpu.VMEM((2, XL, chunk), BF16),
            pltpu.VMEM((count // 128, 128), F32),
        ],
        compiler_params=limit(24 * MIB),
        cost_estimate=pl.CostEstimate(
            flops=slabs * 2 * FIELDS * ROWS * XL * count, bytes_accessed=1_000_000, transcendentals=0
        ),
    )(step_size, target, cells, velocity, mesh)


def total_kernel(scale, *refs):
    grads, outs = refs[:-3], refs[-3:]
    total = grads[0][...]
    for other in grads[1:]:
        total = total + other[...]
    total = total * scale
    for first, out in zip((0, 8, 16), outs):
        out[...] = total[first : first + out.shape[0], 0 : out.shape[1]]


def add_up(grads, weights, scale):
    return pl.pallas_call(
        functools.partial(total_kernel, scale),
        in_specs=[VMEM] * len(grads),
        out_specs=[VMEM] * 3,
        out_shape=[jax.ShapeDtypeStruct(w.shape, F32) for w in weights],
        compiler_params=limit(4 * MIB),
    )(*grads)


def shifted(value, axis, distance):
    count = lax.axis_size(axis)
    return lax.ppermute(value, axis, [(i, (i + distance) % count) for i in range(count)])


def from_all(value, axis):
    count = lax.axis_size(axis)
    others = []
    for k in range(1, count):
        if count & (count - 1):
            others.append(shifted(value, axis, -k))
        else:
            others.append(lax.ppermute(value, axis, [(i, i ^ k) for i in range(count)]))
    return [value] + others


def local(masses, velocity, dest_slab, dest_cell, w_first, w_middle, w_last, step_size, cotangent):
    slabs = lax.axis_size("slab")
    column = ("pencil", "sub")
    count = masses.shape[0]
    dense = (count // 128, 128)
    target, cells = dest_slab.reshape(dense), dest_cell.reshape(dense)
    message = pack(step_size, masses.reshape(dense), target, cells, cotangent, slabs)
    messages = from_all(message, "slab")
    painted = None
    for number, message in enumerate(messages):
        painted = paint(painted, message, dense[0], slabs, number == slabs - 1)
        painted = painted[0] if number < slabs - 1 else painted
    low, high = painted
    low, w_first, w_middle, w_last = lax.optimization_barrier((low, w_first, w_middle, w_last))
    before, after = shifted(high, column, 1), shifted(low, column, -1)
    band_list = bands(w_first, w_middle, w_last)
    mesh, grads = network((low, high, after, before), band_list, w_middle.shape[0], slabs)
    all_grads = from_all(grads, column)
    velocity_new, grad_mass = read_out(step_size, target, cells, velocity, mesh, slabs)
    cell_total = ZL * YL * XL * slabs * lax.axis_size("pencil") * lax.axis_size("sub")
    weight_grads = add_up(all_grads, (w_first, w_middle, w_last), 1.0 / math.sqrt(cell_total))
    return (velocity_new, grad_mass.reshape(count), *weight_grads)


def solution(mesh):
    everywhere = ("runs", "slab", "pencil", "sub")
    placed = (
        P(everywhere),
        P(None, everywhere),
        P(everywhere, None),
        P(everywhere),
        P(),
        P(),
        P(),
        P(),
        P(None, everywhere),
    )
    return jax.shard_map(
        local,
        mesh=mesh,
        in_specs=placed,
        out_specs=(
            P(None, everywhere),
            P(everywhere),
            P("runs", None),
            P("runs", None),
            P("runs", None),
        ),
        check_vma=False,
    )
```

```python
import functools
import math

import jax
import jax.numpy as jnp
import numpy as np
from jax import lax
from jax.experimental import pallas as pl
from jax.experimental.pallas import tpu as pltpu
from jax.sharding import PartitionSpec as P

ZL = 4
YL = 8
XL = 256
ROWS = ZL * YL
FIELDS = 4
POS = 16
HALF = POS // 4
BF16 = jnp.bfloat16
F32 = jnp.float32
NT = (((1,), (1,)), ((), ()))
MIB = 1024 * 1024
VMEM = pl.BlockSpec(memory_space=pltpu.VMEM)
SMEM = pl.BlockSpec(memory_space=pltpu.SMEM)


def dot(a, b):
    return jnp.dot(a, b, preferred_element_type=F32)


def dot_nt(a, b):
    return lax.dot_general(a, b, NT, preferred_element_type=F32)


def row_iota(shape, dim):
    return lax.broadcasted_iota(jnp.int32, shape, dim)


def limit(size):
    return pltpu.CompilerParams(vmem_limit_bytes=size)


def pack_kernel(step_ref, mass_ref, slab_ref, cell_ref, cot_ref, *rest):
    outs, rows = rest[:-1], rest[-1]
    tiles = mass_ref.shape[0]
    cell, slab = cell_ref[...], slab_ref[...]
    z, y = cell >> 11, (cell >> 8) & 7
    code = ((slab & 7) << 5) + ((y >> 2) << 4) + (z << 2) + (y & 3)
    for component in range(3):
        for t in range(tiles):
            row = component * tiles + t
            rows[row : row + 1, :] = cot_ref[component : component + 1, t * 128 : (t + 1) * 128]
    parts = [
        mass_ref[...],
        (step_ref[0] * rows[...]).astype(BF16),
        code.astype(F32).astype(BF16),
        (cell & (XL - 1)).astype(F32).astype(BF16),
        (slab >> 3).astype(F32).astype(BF16),
    ]
    for out_ref in outs:
        first = 0
        for part in parts:
            if first < out_ref.shape[0]:
                out_ref[first : first + part.shape[0], :] = part
            first += part.shape[0]


def pack(step_size, masses, target, cells, cotangent, slabs):
    tiles = masses.shape[0]
    shape = jax.ShapeDtypeStruct(((6 if slabs <= 8 else 7) * tiles, 128), BF16)
    return pl.pallas_call(
        pack_kernel,
        in_specs=[SMEM] + [VMEM] * 4,
        out_specs=[VMEM] * slabs,
        out_shape=[shape] * slabs,
        scratch_shapes=[pltpu.VMEM((3 * tiles, 128), F32)],
        compiler_params=limit(60 * MIB),
    )(step_size, masses, target, cells, cotangent)


def spread_rows(dense, height, first, count):
    tiles = [
        jnp.broadcast_to(dense[t : t + 1, :], (height, 128)) for t in range(first, first + count)
    ]
    return jnp.concatenate(tiles, axis=1)


def fill_lane_hot(store, lane, chunk):
    sixteen = row_iota((16, chunk), 0)
    zero, one = jnp.zeros((16, chunk), BF16), jnp.ones((16, chunk), BF16)
    for group in range(XL // 16):
        same = lane == (sixteen + 16 * group).astype(F32).astype(BF16)
        store[16 * group : 16 * group + 16, :] = jnp.where(same, one, zero)


def paint_kernel(slabs, chunk, tiles, started, final, count, *refs):
    before, refs = (refs[0], refs[1:]) if started else (None, refs)
    messages, refs = refs[:count], refs[count:]
    outs, (hot, lane_hot, total) = refs[:-3], refs[-3:]
    step = chunk // 128
    sixteen = row_iota((16, chunk), 0)
    zero = jnp.zeros((16, chunk), BF16)
    for number in range(count * (tiles // step)):
        message, turn = messages[number // (tiles // step)], number % (tiles // step)
        here, here_lane = hot.at[turn % 2], lane_hot.at[turn % 2]

        def spread(field):
            rows = message[field * tiles : (field + 1) * tiles, :].astype(F32)
            return spread_rows(rows, 16, turn * step, step)

        fill_lane_hot(here_lane, spread(5).astype(BF16), chunk)
        values = [spread(field).astype(BF16) for field in range(FIELDS)]
        code = spread(4)
        for eight in range(0, slabs, 8):
            code_tile = code if slabs <= 8 else jnp.where(spread(6) == eight // 8, code, -1.0)
            code_tile = code_tile.astype(BF16)
            for slab in range(eight, min(eight + 8, slabs)):
                for half in range(2):
                    place = ((slab - eight) * 2 + half) * 16
                    same = code_tile == (sixteen + place).astype(F32).astype(BF16)
                    for field in range(FIELDS):
                        first = ((half * FIELDS + field) * slabs + slab) * 16
                        here[first : first + 16, :] = jnp.where(same, values[field], zero)
        part = dot_nt(here[...], here_lane[...])
        if number > 0:
            total[...] += part
        elif started:
            total[...] = before[...] + part
        else:
            total[...] = part
    if final:
        middle = total.shape[0] // 2
        outs[0][...] = total[:middle, :].astype(BF16)
        outs[1][...] = total[middle:, :].astype(BF16)
    else:
        outs[0][...] = total[...]


def paint(before, messages, tiles, slabs, final):
    chunk = 128 * math.gcd(tiles, 16)
    height = 2 * FIELDS * slabs * 16
    scratch = 2 * chunk * (height + XL) * 2 + height * XL * 4
    shapes = [jax.ShapeDtypeStruct((height, XL), F32)]
    if final:
        shapes = [jax.ShapeDtypeStruct((height // 2, XL), BF16)] * 2
    given = messages if before is None else [before] + messages
    return pl.pallas_call(
        functools.partial(
            paint_kernel, slabs, chunk, tiles, before is not None, final, len(messages)
        ),
        in_specs=[VMEM] * len(given),
        out_specs=[VMEM] * len(shapes),
        out_shape=shapes,
        scratch_shapes=[
            pltpu.VMEM((2, height, chunk), BF16),
            pltpu.VMEM((2, XL, chunk), BF16),
            pltpu.VMEM((height, XL), F32),
        ],
        compiler_params=limit(scratch + height * XL * 24 + 12 * MIB),
        cost_estimate=pl.CostEstimate(
            flops=2 * height * XL * tiles * 128 * len(messages), bytes_accessed=MIB, transcendentals=0
        ),
    )(*given)


def y_of(place):
    rest = place - 8
    if isinstance(place, np.ndarray):
        return np.where(place < 8, place + 4, np.where(rest % 2 == 0, 12 + rest // 2, 3 - rest // 2))
    halo = jnp.where((rest & 1) == 0, 12 + (rest >> 1), 3 - (rest >> 1))
    return jnp.where(place < 8, place + 4, halo)


def columns(rows, channels):
    col = np.arange(9 * rows * channels)
    pair, place, channel = col // (rows * channels), col // channels % rows, col % channels
    taps = [((pair // 3 * 3 + b) * 3 + pair % 3) * channels + channel for b in range(3)]
    return np.stack(taps + [y_of(place)] + [np.zeros_like(col)] * 4).astype(np.int32)


def window_columns(rows, channels):
    col = np.arange(3 * rows * channels)
    listed = [y_of(col // channels % rows), col // (rows * channels) * channels + col % channels]
    return np.stack(listed + [np.zeros_like(col)] * 6).astype(np.int32)


def band(weight, table, row_channel, row_place):
    outs, count = weight.shape
    width = table.shape[1]
    rows = row_channel.shape[0]
    pick = jnp.where(row_channel[:, 0:outs] == row_iota((rows, outs), 1), 1.0, 0.0)
    spread = dot(pick.astype(BF16), weight).astype(BF16)
    distance = table[3:4, :] - y_of(row_place)
    result = jnp.zeros((rows, width), F32)
    for b in range(3):
        same = row_iota((count, width), 0) == table[b : b + 1, :]
        picked = dot(spread, jnp.where(same, 1.0, 0.0).astype(BF16))
        result = jnp.where(distance == b - 1, picked, result)
    return result


def band_kernel(
    first_ref, middle_ref, last_ref, c1_ref, c2_ref, c3_ref,
    b1_ref, b2_ref, b3_ref, t1_ref, t2_ref, t3_ref,
):
    channels = first_ref.shape[0]
    bits = channels.bit_length() - 1

    def mixed(rows, width):
        row = row_iota((rows, width), 0)
        return row & (channels - 1), row >> bits

    def turned(full, pair, width, rows, out_ref):
        block = full[:, pair * width : (pair + 1) * width].T[0:rows].astype(BF16)
        out_ref[:, (8 - pair) * block.shape[1] : (9 - pair) * block.shape[1]] = block

    def stack(out_ref, pair, block):
        rows, width = block.shape
        first = pair % 3 * width
        out_ref[pair // 3 * rows : (pair // 3 + 1) * rows, first : first + width] = block

    rows = b1_ref.shape[0]
    table = c1_ref[...]
    full = band(first_ref[...], table, mixed(rows, 128)[0], mixed(rows, table.shape[1])[1])
    b1_ref[...] = full.astype(BF16)
    short = t1_ref.shape[1] // 3
    for pair in range(9):
        stack(t1_ref, 8 - pair, full[0:short, pair * POS : (pair + 1) * POS].T.astype(BF16))
    rows = b2_ref.shape[0]
    table = c2_ref[...]
    full = band(middle_ref[...], table, mixed(rows, 128)[0], mixed(rows, table.shape[1])[1])
    b2_ref[...] = full.astype(BF16)
    for pair in range(9):
        turned(full, pair, full.shape[1] // 9, t2_ref.shape[0], t2_ref)
    rows = 3 * POS
    table = c3_ref[...]
    channel = row_iota((rows, 128), 0) >> 4
    full = band(last_ref[...], table, channel, row_iota((rows, table.shape[1]), 0) & (POS - 1))
    width, short = full.shape[1] // 9, b3_ref.shape[1] // 3
    own = [full[o * POS : o * POS + YL] for o in range(3)] + [jnp.zeros((YL, full.shape[1]), F32)]
    own = jnp.concatenate(own, axis=0).astype(BF16)
    for pair in range(9):
        stack(b3_ref, pair, own[:, pair * width : pair * width + short])
        turned(full, pair, width, t3_ref.shape[0], t3_ref)


def bands(w_first, w_middle, w_last):
    c = w_middle.shape[0]
    tables = [jnp.asarray(t) for t in (columns(16, 1), columns(14, c), columns(12, c))]
    shapes = [
        (14 * c, 9 * 16), (12 * c, 9 * 14 * c), (3 * 4 * YL, 3 * 10 * c),
        (3 * POS, 3 * 10 * c), (10 * c, 9 * 12 * c), (12 * c, 9 * 3 * POS),
    ]
    return pl.pallas_call(
        band_kernel,
        in_specs=[VMEM] * 6,
        out_specs=[VMEM] * 6,
        out_shape=[jax.ShapeDtypeStruct(s, BF16) for s in shapes],
        compiler_params=limit(20 * MIB),
        cost_estimate=pl.CostEstimate(
            flops=800_000_000, bytes_accessed=4_000_000, transcendentals=0
        ),
    )(w_first, w_middle, w_last, *tables)


def slope(pre, sigma):
    return sigma * (1.0 + pre * (1.0 - sigma))


def split_three(value):
    high = value.astype(BF16).astype(F32)
    rest = value - high
    mid = rest.astype(BF16).astype(F32)
    return jnp.concatenate([high, mid, rest - mid], axis=0).astype(BF16)


def weight_sum(full, table, channels, mixed, outs):
    count, width = full.shape[0] // 3, full.shape[1]
    group = row_iota((3 * channels, width), 0) == table[1:2, :]
    group = jnp.where(group, 1.0, 0.0).astype(BF16)
    picked = []
    for b in range(3):
        for e in range(3):
            block = full[e * count : (e + 1) * count, :]
            if mixed:
                parts = [
                    jnp.where(table[0:1, :] == place + 3 + b, block[place * 8 : place * 8 + 8, :], 0.0)
                    for place in range(YL)
                ]
                picked.append(functools.reduce(jnp.add, parts))
                continue
            wanted = table[0:1, :] - row_iota((YL, width), 0) == 3 + b
            rows = [
                jnp.sum(
                    jnp.where(wanted, block[o * POS : o * POS + YL, :], 0.0), axis=0, keepdims=True
                )
                for o in range(outs)
            ]
            picked.append(jnp.concatenate(rows + [jnp.zeros_like(rows[0])] * (8 - outs), axis=0))
    parts = dot_nt(split_three(jnp.concatenate(picked, axis=0)), group)
    total = parts[0:72] + parts[72:144] + parts[144:216]
    pieces = [
        total[pair * 8 : pair * 8 + 8, a * channels : (a + 1) * channels]
        for a in range(3)
        for pair in range(9)
    ]
    return jnp.concatenate(pieces, axis=1)


class Store:
    def __init__(self, ref, depth, rows):
        self.ref, self.depth, self.rows = ref, depth, rows

    def put(self, plane, value, first=0):
        places = [plane + 1]
        if plane == 0:
            places.append(self.depth + 1)
        if plane == self.depth - 1:
            places.append(0)
        for e, shift in enumerate((1, 0, XL - 1)):
            moved = (value if shift == 0 else pltpu.roll(value, shift, 1)).astype(BF16)
            for place in places:
                row = (place * 3 + e) * self.rows + first
                self.ref[row : row + value.shape[0], :] = moved

    def window(self, plane):
        return self.ref[plane * 3 * self.rows : (plane + 3) * 3 * self.rows, :]

    def plane(self, plane):
        return self.ref[(plane + 1) * 3 * self.rows : (plane + 2) * 3 * self.rows, :]

    def shifted(self, plane, e, count):
        row = ((plane + 1) * 3 + e) * self.rows
        return self.ref[row : row + count, :]


def product(delta, count, source, plane):
    planes = range(plane, plane + 4)
    left = [
        jnp.concatenate([delta.shifted(p, e, count) for e in (2, 1, 0)], axis=0) for p in planes
    ]
    right = [
        jnp.concatenate([source.shifted(p + a, 1, source.rows) for a in (-1, 0, 1)], axis=0)
        for p in planes
    ]
    return dot_nt(jnp.concatenate(left, axis=1), jnp.concatenate(right, axis=1))


class Plan:
    def __init__(self):
        self.stages = {}

    def add(self, stage, key, after, step):
        self.stages.setdefault(stage, []).append((key, after, step))

    def in_turn(self):
        for steps in self.stages.values():
            for _, _, step in steps:
                step()


def net_kernel(
    slabs, channels, shared,
    low_ref, high_ref, after_ref, before_ref,
    b1_ref, b2_ref, b3_ref, t1_ref, t2_ref, t3_ref, order_ref, c1_ref, c2_ref, c3_ref,
    mesh_ref, grads_ref,
    s0_ref, sg_ref, a_ref, b_ref, slope1, slope2, fields, *more,
):
    depth = slabs * ZL
    s0, sg = Store(s0_ref, depth, POS), Store(sg_ref, depth, 3 * POS)
    s1, s2 = Store(a_ref, depth, 14 * channels), Store(b_ref, depth, 10 * channels)
    d2 = Store(b_ref if shared else more[0], depth, 12 * channels)
    d1 = Store(a_ref if shared else more[1], depth, 10 * channels)
    order = order_ref[...]
    grads_ref[...] = jnp.zeros_like(grads_ref)
    inner = 10 * channels
    plan, kept, sums = Plan(), {}, {}

    def near(stage, plane):
        return [(stage, (plane + a) % depth) for a in (-1, 0, 1)]

    def place(plane, field):
        first = (plane // ZL * FIELDS + field) * ROWS + plane % ZL * YL
        return slice(first, first + YL)

    def load(slab):
        for c in range(FIELDS):
            first = (c * slabs + slab) * 16
            pieces = [ref[first : first + 16, :] for ref in (low_ref, high_ref, after_ref, before_ref)]
            rows = dot(order, jnp.concatenate(pieces, axis=0))
            for z in range(ZL):
                value = rows[z * POS : (z + 1) * POS, :]
                if c == 0:
                    s0.put(slab * ZL + z, value)
                else:
                    sg.put(slab * ZL + z, value, (c - 1) * POS)

    def first_layer(plane):
        pre = dot(b1_ref[...], s0.window(plane))
        sigma = jax.nn.sigmoid(pre)
        s1.put(plane, pre * sigma)
        slope1[plane] = slope(pre[0:inner], sigma[0:inner])

    def second_layer(plane):
        pre = dot(b2_ref[...], s1.window(plane))
        sigma = jax.nn.sigmoid(pre)
        s2.put(plane, pre[0:inner] * sigma[0:inner])
        slope2[plane] = slope(pre, sigma)

    def stacked(stage, weight_ref, store, plane):
        kept[stage, plane] = dot(weight_ref[...], store.plane(plane))

    def unstacked(stage, plane):
        rows = kept[stage, plane].shape[0] // 3
        return functools.reduce(
            jnp.add,
            [kept[key][a * rows : (a + 1) * rows] for a, key in enumerate(near(stage, plane))],
        )

    def force(plane):
        value = unstacked("force parts", plane)
        for c in range(3):
            fields[place(plane, c), :] = value[c * YL : (c + 1) * YL, :]

    def pull(plane):
        fields[place(plane, 3), :] = unstacked("pull parts", plane)[0:YL, :]

    def second_delta(plane):
        d2.put(plane, dot(t3_ref[...], sg.window(plane)) * slope2[plane])

    def first_delta(plane):
        d1.put(plane, dot(t2_ref[...], d2.window(plane)) * slope1[plane])

    def add_product(name, delta, count, source, plane):
        term = product(delta, count, source, plane)
        sums[name] = sums[name] + term if name in sums else term

    def bind(step, *given):
        return functools.partial(step, *given)

    for slab in range(slabs):
        plan.add("load", slab, [], bind(load, slab))
    for p in range(depth):
        slabs_near = [("load", q // ZL) for _, q in near("", p)]
        plan.add("first", p, slabs_near, bind(first_layer, p))
    for p in range(depth):
        plan.add("second", p, near("first", p), bind(second_layer, p))
    for p in range(depth):
        plan.add("force parts", p, [("second", p)], bind(stacked, "force parts", b3_ref, s2, p))
    for p in range(depth):
        plan.add("force", p, near("force parts", p), bind(force, p))
    groups = range(0, depth, 4)
    for p in groups:
        after = [("second", q % depth) for q in range(p - 1, p + 5)]
        plan.add("last sum", p, after, bind(add_product, "last", sg, 3 * POS, s2, p))
    for p in range(depth):
        plan.add("second delta", p, [("second", p)], bind(second_delta, p))
    for p in groups:
        after = [("second delta", q) for q in range(p, p + 4)]
        plan.add("middle sum", p, after, bind(add_product, "middle", d2, YL * channels, s1, p))
    for p in range(depth):
        plan.add("first delta", p, near("second delta", p), bind(first_delta, p))
    for p in groups:
        after = [("first delta", q) for q in range(p, p + 4)]
        plan.add("first sum", p, after, bind(add_product, "first", d1, YL * channels, s0, p))
    for p in range(depth):
        plan.add("pull parts", p, [("first delta", p)], bind(stacked, "pull parts", t1_ref, d1, p))
    for p in range(depth):
        plan.add("pull", p, near("pull parts", p), bind(pull, p))
    plan.in_turn()
    mesh_ref[...] = fields[...].astype(BF16)
    for first, name, table_ref, ins, mixed in (
        (0, "first", c1_ref, 1, True),
        (8, "middle", c2_ref, channels, True),
        (16, "last", c3_ref, channels, False),
    ):
        outs = channels if mixed else 3
        grads_ref[first : first + 8, 0 : 27 * ins] = weight_sum(
            sums[name], table_ref[...], ins, mixed, outs
        )


def network(halves, band_list, channels, slabs):
    depth = slabs * ZL
    order = np.zeros((64, 64), np.float32)
    for z in range(4):
        for y in range(4):
            for h, place in enumerate((y, 4 + y, 8 + 2 * y, 15 - 2 * y)):
                order[z * 16 + place, h * 16 + z * 4 + y] = 1.0
    planes = 3 * (depth + 2)
    shared = slabs > 4
    sizes = [POS, 3 * POS, 14 * channels, (12 if shared else 10) * channels]
    stores = [pltpu.VMEM((planes * n, XL), BF16) for n in sizes]
    more = [] if shared else [12 * channels, 10 * channels]
    slopes = [pltpu.VMEM((depth, n * channels, XL), F32) for n in (10, 12)]
    size = sum(sizes + more) * planes * XL * 2 + (22 * channels + 32) * depth * XL * 4
    tables = [jnp.asarray(t) for t in (window_columns(16, 1), window_columns(14, channels), window_columns(10, channels))]
    given = (*halves, *band_list, jnp.asarray(order, BF16), *tables)
    return pl.pallas_call(
        functools.partial(net_kernel, slabs, channels, shared),
        in_specs=[VMEM] * len(given),
        out_specs=[VMEM] * 2,
        out_shape=[
            jax.ShapeDtypeStruct((slabs * FIELDS * ROWS, XL), BF16),
            jax.ShapeDtypeStruct((24, 256), F32),
        ],
        scratch_shapes=stores
        + slopes
        + [pltpu.VMEM((slabs * FIELDS * ROWS, XL), F32)]
        + [pltpu.VMEM((planes * n, XL), BF16) for n in more],
        compiler_params=limit(size + 12 * MIB),
    )(*given)


def readout_kernel(slabs, chunk, step_ref, slab_ref, cell_ref, velocity_ref, mesh_ref, *rest):
    velocity_out, mass_out, lane_hot, mass_rows = rest
    cell = cell_ref[...]
    code = slab_ref[...] * ROWS + (cell >> 8)
    lanes = (cell & (XL - 1)).astype(F32)
    eight = row_iota((8, chunk), 0)
    tiles = chunk // 128
    height = FIELDS * ROWS
    for turn in range(cell.shape[0] // tiles):
        here = lane_hot.at[turn % 2]
        fill_lane_hot(here, spread_rows(lanes, 16, turn * tiles, tiles).astype(BF16), chunk)
        code_tile = spread_rows(code, 8, turn * tiles, tiles)
        sums = [jnp.zeros((8, chunk), F32) for _ in range(FIELDS)]
        everything = dot(mesh_ref[...], here[...])
        for k in range(slabs):
            rows = everything[k * height : (k + 1) * height, :]
            for group in range(ROWS // 8):
                same = code_tile == eight + (k * ROWS + group * 8)
                for c in range(FIELDS):
                    first = c * ROWS + group * 8
                    sums[c] = sums[c] + jnp.where(same, rows[first : first + 8, :], 0.0)
        span = slice(turn * chunk, (turn + 1) * chunk)
        for c in range(3):
            force = jnp.sum(sums[c], axis=0, keepdims=True)
            velocity_out[c : c + 1, span] = velocity_ref[c : c + 1, span] + step_ref[0] * force
        pull = jnp.sum(sums[3], axis=0, keepdims=True)
        for t in range(tiles):
            mass_rows[turn * tiles + t : turn * tiles + t + 1, :] = pull[:, t * 128 : (t + 1) * 128]
    mass_out[...] = mass_rows[...].astype(BF16)


def read_out(step_size, target, cells, velocity, mesh, slabs):
    count = velocity.shape[1]
    chunk = math.gcd(count, 1024)
    return pl.pallas_call(
        functools.partial(readout_kernel, slabs, chunk),
        in_specs=[SMEM] + [VMEM] * 4,
        out_specs=[VMEM] * 2,
        out_shape=[
            jax.ShapeDtypeStruct((3, count), F32),
            jax.ShapeDtypeStruct((count // 128, 128), BF16),
        ],
        scratch_shapes=[
            pltpu.VMEM((2, XL, chunk), BF16),
            pltpu.VMEM((count // 128, 128), F32),
        ],
        compiler_params=limit((16 + 4 * slabs) * MIB),
        cost_estimate=pl.CostEstimate(
            flops=slabs * 2 * FIELDS * ROWS * XL * count, bytes_accessed=1_000_000, transcendentals=0
        ),
    )(step_size, target, cells, velocity, mesh)


def total_kernel(scale, *refs):
    grads, outs = refs[:-3], refs[-3:]
    total = grads[0][...]
    for other in grads[1:]:
        total = total + other[...]
    total = total * scale
    for first, out in zip((0, 8, 16), outs):
        out[...] = total[first : first + out.shape[0], 0 : out.shape[1]]


def add_up(grads, weights, scale):
    return pl.pallas_call(
        functools.partial(total_kernel, scale),
        in_specs=[VMEM] * len(grads),
        out_specs=[VMEM] * 3,
        out_shape=[jax.ShapeDtypeStruct(w.shape, F32) for w in weights],
        compiler_params=limit(4 * MIB),
    )(*grads)


def shifted(value, axis, distance):
    count = lax.axis_size(axis)
    return lax.ppermute(value, axis, [(i, (i + distance) % count) for i in range(count)])


def from_all(value, axis):
    count = lax.axis_size(axis)
    values = value if isinstance(value, (list, tuple)) else [value] * count
    others = []
    order = list(range(1, count))
    if count > 3:
        order = order[1:2] + order[0:1] + order[2:]
    for n, k in enumerate(order, 1):
        if count & (count - 1):
            others.append(shifted(values[n], axis, -k))
        else:
            others.append(lax.ppermute(values[n], axis, [(i, i ^ k) for i in range(count)]))
    return [values[0]] + others


def local(masses, velocity, dest_slab, dest_cell, w_first, w_middle, w_last, step_size, cotangent):
    slabs = lax.axis_size("slab")
    column = ("pencil", "sub")
    count = masses.shape[0]
    dense = (count // 128, 128)
    target, cells = dest_slab.reshape(dense), dest_cell.reshape(dense)
    packed = pack(step_size, masses.reshape(dense), target, cells, cotangent, slabs)
    messages = from_all(packed, "slab")
    painted = None
    for message in messages[:-2]:
        painted = paint(painted, [message], dense[0], slabs, False)[0]
    low, high = paint(painted, messages[-2:], dense[0], slabs, True)
    low, w_first, w_middle, w_last = lax.optimization_barrier((low, w_first, w_middle, w_last))
    before, after = shifted(high, column, 1), shifted(low, column, -1)
    band_list = bands(w_first, w_middle, w_last)
    mesh, grads = network((low, high, after, before), band_list, w_middle.shape[0], slabs)
    all_grads = from_all(grads, column)
    velocity_new, grad_mass = read_out(step_size, target, cells, velocity, mesh, slabs)
    cell_total = ZL * YL * XL * slabs * lax.axis_size("pencil") * lax.axis_size("sub")
    weight_grads = add_up(all_grads, (w_first, w_middle, w_last), 1.0 / math.sqrt(cell_total))
    return (velocity_new, grad_mass.reshape(count), *weight_grads)


def solution(mesh):
    everywhere = ("runs", "slab", "pencil", "sub")
    placed = (
        P(everywhere),
        P(None, everywhere),
        P(everywhere, None),
        P(everywhere),
        P(),
        P(),
        P(),
        P(),
        P(None, everywhere),
    )
    return jax.shard_map(
        local,
        mesh=mesh,
        in_specs=placed,
        out_specs=(
            P(None, everywhere),
            P(everywhere),
            P("runs", None),
            P("runs", None),
            P("runs", None),
        ),
        check_vma=False,
    )
```

```python
import functools
import math

import jax
import jax.numpy as jnp
import numpy as np
from jax import lax
from jax.experimental import pallas as pl
from jax.experimental.pallas import tpu as pltpu
from jax.sharding import PartitionSpec as P

ZL = 4
YL = 8
XL = 256
ROWS = ZL * YL
FIELDS = 4
POS = 16
HALF = POS // 4
BF16 = jnp.bfloat16
F32 = jnp.float32
NT = (((1,), (1,)), ((), ()))
MIB = 1024 * 1024
VMEM = pl.BlockSpec(memory_space=pltpu.VMEM)
SMEM = pl.BlockSpec(memory_space=pltpu.SMEM)


def dot(a, b):
    return jnp.dot(a, b, preferred_element_type=F32)


def dot_nt(a, b):
    return lax.dot_general(a, b, NT, preferred_element_type=F32)


def row_iota(shape, dim):
    return lax.broadcasted_iota(jnp.int32, shape, dim)


def limit(size):
    return pltpu.CompilerParams(vmem_limit_bytes=size)


def pack_kernel(step_ref, mass_ref, slab_ref, cell_ref, cot_ref, *rest):
    outs, rows = rest[:-1], rest[-1]
    tiles = mass_ref.shape[0]
    cell, slab = cell_ref[...], slab_ref[...]
    z, y = cell >> 11, (cell >> 8) & 7
    code = ((slab & 7) << 5) + ((y >> 2) << 4) + (z << 2) + (y & 3)
    for component in range(3):
        for t in range(tiles):
            row = component * tiles + t
            rows[row : row + 1, :] = cot_ref[component : component + 1, t * 128 : (t + 1) * 128]
    parts = [
        mass_ref[...],
        (step_ref[0] * rows[...]).astype(BF16),
        code.astype(F32).astype(BF16),
        (cell & (XL - 1)).astype(F32).astype(BF16),
        (slab >> 3).astype(F32).astype(BF16),
    ]
    for out_ref in outs:
        first = 0
        for part in parts:
            if first < out_ref.shape[0]:
                out_ref[first : first + part.shape[0], :] = part
            first += part.shape[0]


def pack(step_size, masses, target, cells, cotangent, slabs):
    tiles = masses.shape[0]
    shape = jax.ShapeDtypeStruct(((6 if slabs <= 8 else 7) * tiles, 128), BF16)
    return pl.pallas_call(
        pack_kernel,
        in_specs=[SMEM] + [VMEM] * 4,
        out_specs=[VMEM] * slabs,
        out_shape=[shape] * slabs,
        scratch_shapes=[pltpu.VMEM((3 * tiles, 128), F32)],
        compiler_params=limit(60 * MIB),
    )(step_size, masses, target, cells, cotangent)


def spread_rows(dense, height, first, count):
    tiles = [
        jnp.broadcast_to(dense[t : t + 1, :], (height, 128)) for t in range(first, first + count)
    ]
    return jnp.concatenate(tiles, axis=1)


def fill_lane_hot(store, lane, chunk):
    sixteen = row_iota((16, chunk), 0)
    zero, one = jnp.zeros((16, chunk), BF16), jnp.ones((16, chunk), BF16)
    for group in range(XL // 16):
        same = lane == (sixteen + 16 * group).astype(F32).astype(BF16)
        store[16 * group : 16 * group + 16, :] = jnp.where(same, one, zero)


def paint_kernel(slabs, chunk, tiles, started, halves, count, *refs):
    before, refs = (refs[0], refs[1:]) if started else (None, refs)
    messages, refs = refs[:count], refs[count:]
    outs, (hot, lane_hot, total) = refs[:-3], refs[-3:]
    step = chunk // 128
    sixteen = row_iota((16, chunk), 0)
    zero = jnp.zeros((16, chunk), BF16)
    for number in range(count * (tiles // step)):
        message, turn = messages[number // (tiles // step)], number % (tiles // step)
        here, here_lane = hot.at[turn % 2], lane_hot.at[turn % 2]

        def spread(field):
            rows = message[field * tiles : (field + 1) * tiles, :].astype(F32)
            return spread_rows(rows, 16, turn * step, step)

        fill_lane_hot(here_lane, spread(5).astype(BF16), chunk)
        values = [spread(field).astype(BF16) for field in range(FIELDS)]
        code = spread(4)
        for eight in range(0, slabs, 8):
            code_tile = code if slabs <= 8 else jnp.where(spread(6) == eight // 8, code, -1.0)
            code_tile = code_tile.astype(BF16)
            for slab in range(eight, min(eight + 8, slabs)):
                for number_of, half in enumerate(halves):
                    place = ((slab - eight) * 2 + half) * 16
                    same = code_tile == (sixteen + place).astype(F32).astype(BF16)
                    for field in range(FIELDS):
                        first = ((number_of * FIELDS + field) * slabs + slab) * 16
                        here[first : first + 16, :] = jnp.where(same, values[field], zero)
        part = dot_nt(here[...], here_lane[...])
        if number > 0:
            total[...] += part
        elif started:
            skip = before.shape[0] - total.shape[0] if halves[0] else 0
            total[...] = before[skip : skip + total.shape[0], :] + part
        else:
            total[...] = part
    outs[0][...] = total[...].astype(outs[0].dtype)


def paint(before, messages, tiles, slabs, half=None):
    chunk = 128 * math.gcd(tiles, 16)
    halves = (0, 1) if half is None else (half,)
    height = len(halves) * FIELDS * slabs * 16
    scratch = 2 * chunk * (height + XL) * 2 + height * XL * 4
    shapes = [jax.ShapeDtypeStruct((height, XL), F32 if half is None else BF16)]
    given = messages if before is None else [before] + messages
    return pl.pallas_call(
        functools.partial(
            paint_kernel, slabs, chunk, tiles, before is not None, halves, len(messages)
        ),
        in_specs=[VMEM] * len(given),
        out_specs=[VMEM] * len(shapes),
        out_shape=shapes,
        scratch_shapes=[
            pltpu.VMEM((2, height, chunk), BF16),
            pltpu.VMEM((2, XL, chunk), BF16),
            pltpu.VMEM((height, XL), F32),
        ],
        compiler_params=limit(scratch + height * XL * 24 + 12 * MIB),
        cost_estimate=pl.CostEstimate(
            flops=2 * height * XL * tiles * 128 * len(messages), bytes_accessed=MIB, transcendentals=0
        ),
    )(*given)[0]


def y_of(place):
    rest = place - 8
    if isinstance(place, np.ndarray):
        return np.where(place < 8, place + 4, np.where(rest % 2 == 0, 12 + rest // 2, 3 - rest // 2))
    halo = jnp.where((rest & 1) == 0, 12 + (rest >> 1), 3 - (rest >> 1))
    return jnp.where(place < 8, place + 4, halo)


def columns(rows, channels):
    col = np.arange(9 * rows * channels)
    pair, place, channel = col // (rows * channels), col // channels % rows, col % channels
    taps = [((pair // 3 * 3 + b) * 3 + pair % 3) * channels + channel for b in range(3)]
    return np.stack(taps + [y_of(place)] + [np.zeros_like(col)] * 4).astype(np.int32)


def window_columns(rows, channels):
    col = np.arange(3 * rows * channels)
    listed = [y_of(col // channels % rows), col // (rows * channels) * channels + col % channels]
    return np.stack(listed + [np.zeros_like(col)] * 6).astype(np.int32)


def band(weight, table, row_channel, row_place):
    outs, count = weight.shape
    width = table.shape[1]
    rows = row_channel.shape[0]
    pick = jnp.where(row_channel[:, 0:outs] == row_iota((rows, outs), 1), 1.0, 0.0)
    spread = dot(pick.astype(BF16), weight).astype(BF16)
    distance = table[3:4, :] - y_of(row_place)
    result = jnp.zeros((rows, width), F32)
    for b in range(3):
        same = row_iota((count, width), 0) == table[b : b + 1, :]
        picked = dot(spread, jnp.where(same, 1.0, 0.0).astype(BF16))
        result = jnp.where(distance == b - 1, picked, result)
    return result


def band_kernel(
    first_ref, middle_ref, last_ref, c1_ref, c2_ref, c3_ref,
    b1_ref, b2_ref, b3_ref, t1_ref, t2_ref, t3_ref,
):
    channels = first_ref.shape[0]
    bits = channels.bit_length() - 1

    def mixed(rows, width):
        row = row_iota((rows, width), 0)
        return row & (channels - 1), row >> bits

    def turned(full, pair, width, rows, out_ref):
        block = full[:, pair * width : (pair + 1) * width].T[0:rows].astype(BF16)
        out_ref[:, (8 - pair) * block.shape[1] : (9 - pair) * block.shape[1]] = block

    def stack(out_ref, pair, block):
        rows, width = block.shape
        first = pair % 3 * width
        out_ref[pair // 3 * rows : (pair // 3 + 1) * rows, first : first + width] = block

    rows = b1_ref.shape[0]
    table = c1_ref[...]
    full = band(first_ref[...], table, mixed(rows, 128)[0], mixed(rows, table.shape[1])[1])
    b1_ref[...] = full.astype(BF16)
    short = t1_ref.shape[1] // 3
    for pair in range(9):
        stack(t1_ref, 8 - pair, full[0:short, pair * POS : (pair + 1) * POS].T.astype(BF16))
    rows = b2_ref.shape[0]
    table = c2_ref[...]
    full = band(middle_ref[...], table, mixed(rows, 128)[0], mixed(rows, table.shape[1])[1])
    b2_ref[...] = full.astype(BF16)
    for pair in range(9):
        turned(full, pair, full.shape[1] // 9, t2_ref.shape[0], t2_ref)
    rows = 3 * POS
    table = c3_ref[...]
    channel = row_iota((rows, 128), 0) >> 4
    full = band(last_ref[...], table, channel, row_iota((rows, table.shape[1]), 0) & (POS - 1))
    width, short = full.shape[1] // 9, b3_ref.shape[1] // 3
    own = [full[o * POS : o * POS + YL] for o in range(3)] + [jnp.zeros((YL, full.shape[1]), F32)]
    own = jnp.concatenate(own, axis=0).astype(BF16)
    for pair in range(9):
        stack(b3_ref, pair, own[:, pair * width : pair * width + short])
        turned(full, pair, width, t3_ref.shape[0], t3_ref)


def bands(w_first, w_middle, w_last):
    c = w_middle.shape[0]
    tables = [jnp.asarray(t) for t in (columns(16, 1), columns(14, c), columns(12, c))]
    shapes = [
        (14 * c, 9 * 16), (12 * c, 9 * 14 * c), (3 * 4 * YL, 3 * 10 * c),
        (3 * POS, 3 * 10 * c), (10 * c, 9 * 12 * c), (12 * c, 9 * 3 * POS),
    ]
    return pl.pallas_call(
        band_kernel,
        in_specs=[VMEM] * 6,
        out_specs=[VMEM] * 6,
        out_shape=[jax.ShapeDtypeStruct(s, BF16) for s in shapes],
        compiler_params=limit(20 * MIB),
        cost_estimate=pl.CostEstimate(
            flops=800_000_000, bytes_accessed=4_000_000, transcendentals=0
        ),
    )(w_first, w_middle, w_last, *tables)


def slope(pre, sigma):
    return sigma * (1.0 + pre * (1.0 - sigma))


def split_three(value):
    high = value.astype(BF16).astype(F32)
    rest = value - high
    mid = rest.astype(BF16).astype(F32)
    return jnp.concatenate([high, mid, rest - mid], axis=0).astype(BF16)


def weight_sum(full, table, channels, mixed, outs):
    count, width = full.shape[0] // 3, full.shape[1]
    group = row_iota((3 * channels, width), 0) == table[1:2, :]
    group = jnp.where(group, 1.0, 0.0).astype(BF16)
    picked = []
    for b in range(3):
        for e in range(3):
            block = full[e * count : (e + 1) * count, :]
            if mixed:
                parts = [
                    jnp.where(table[0:1, :] == place + 3 + b, block[place * 8 : place * 8 + 8, :], 0.0)
                    for place in range(YL)
                ]
                picked.append(functools.reduce(jnp.add, parts))
                continue
            wanted = table[0:1, :] - row_iota((YL, width), 0) == 3 + b
            rows = [
                jnp.sum(
                    jnp.where(wanted, block[o * POS : o * POS + YL, :], 0.0), axis=0, keepdims=True
                )
                for o in range(outs)
            ]
            picked.append(jnp.concatenate(rows + [jnp.zeros_like(rows[0])] * (8 - outs), axis=0))
    parts = dot_nt(split_three(jnp.concatenate(picked, axis=0)), group)
    total = parts[0:72] + parts[72:144] + parts[144:216]
    pieces = [
        total[pair * 8 : pair * 8 + 8, a * channels : (a + 1) * channels]
        for a in range(3)
        for pair in range(9)
    ]
    return jnp.concatenate(pieces, axis=1)


class Store:
    def __init__(self, ref, depth, rows):
        self.ref, self.depth, self.rows = ref, depth, rows

    def put(self, plane, value, first=0):
        places = [plane + 1]
        if plane == 0:
            places.append(self.depth + 1)
        if plane == self.depth - 1:
            places.append(0)
        for e, shift in enumerate((1, 0, XL - 1)):
            moved = (value if shift == 0 else pltpu.roll(value, shift, 1)).astype(BF16)
            for place in places:
                row = (place * 3 + e) * self.rows + first
                self.ref[row : row + value.shape[0], :] = moved

    def window(self, plane):
        return self.ref[plane * 3 * self.rows : (plane + 3) * 3 * self.rows, :]

    def plane(self, plane):
        return self.ref[(plane + 1) * 3 * self.rows : (plane + 2) * 3 * self.rows, :]

    def shifted(self, plane, e, count):
        row = ((plane + 1) * 3 + e) * self.rows
        return self.ref[row : row + count, :]


def product(delta, count, source, plane):
    planes = range(plane, plane + 4)
    left = [
        jnp.concatenate([delta.shifted(p, e, count) for e in (2, 1, 0)], axis=0) for p in planes
    ]
    right = [
        jnp.concatenate([source.shifted(p + a, 1, source.rows) for a in (-1, 0, 1)], axis=0)
        for p in planes
    ]
    return dot_nt(jnp.concatenate(left, axis=1), jnp.concatenate(right, axis=1))


class Plan:
    def __init__(self):
        self.stages = {}

    def add(self, stage, key, after, step):
        self.stages.setdefault(stage, []).append((key, after, step))

    def in_turn(self):
        for steps in self.stages.values():
            for _, _, step in steps:
                step()


def net_kernel(
    slabs, channels, shared,
    low_ref, high_ref, after_ref, before_ref,
    b1_ref, b2_ref, b3_ref, t1_ref, t2_ref, t3_ref, order_ref, c1_ref, c2_ref, c3_ref,
    mesh_ref, grads_ref,
    s0_ref, sg_ref, a_ref, b_ref, slope1, slope2, fields, *more,
):
    depth = slabs * ZL
    s0, sg = Store(s0_ref, depth, POS), Store(sg_ref, depth, 3 * POS)
    s1, s2 = Store(a_ref, depth, 14 * channels), Store(b_ref, depth, 10 * channels)
    d2 = Store(b_ref if shared else more[0], depth, 12 * channels)
    d1 = Store(a_ref if shared else more[1], depth, 10 * channels)
    order = order_ref[...]
    grads_ref[...] = jnp.zeros_like(grads_ref)
    inner = 10 * channels
    plan, kept, sums = Plan(), {}, {}

    def near(stage, plane):
        return [(stage, (plane + a) % depth) for a in (-1, 0, 1)]

    def place(plane, field):
        first = (plane // ZL * FIELDS + field) * ROWS + plane % ZL * YL
        return slice(first, first + YL)

    def load(slab):
        for c in range(FIELDS):
            first = (c * slabs + slab) * 16
            pieces = [ref[first : first + 16, :] for ref in (low_ref, high_ref, after_ref, before_ref)]
            rows = dot(order, jnp.concatenate(pieces, axis=0))
            for z in range(ZL):
                value = rows[z * POS : (z + 1) * POS, :]
                if c == 0:
                    s0.put(slab * ZL + z, value)
                else:
                    sg.put(slab * ZL + z, value, (c - 1) * POS)

    def first_layer(plane):
        pre = dot(b1_ref[...], s0.window(plane))
        sigma = jax.nn.sigmoid(pre)
        s1.put(plane, pre * sigma)
        slope1[plane] = slope(pre[0:inner], sigma[0:inner])

    def second_layer(plane):
        pre = dot(b2_ref[...], s1.window(plane))
        sigma = jax.nn.sigmoid(pre)
        s2.put(plane, pre[0:inner] * sigma[0:inner])
        slope2[plane] = slope(pre, sigma)

    def stacked(stage, weight_ref, store, plane):
        kept[stage, plane] = dot(weight_ref[...], store.plane(plane))

    def unstacked(stage, plane):
        rows = kept[stage, plane].shape[0] // 3
        return functools.reduce(
            jnp.add,
            [kept[key][a * rows : (a + 1) * rows] for a, key in enumerate(near(stage, plane))],
        )

    def force(plane):
        value = unstacked("force parts", plane)
        for c in range(3):
            fields[place(plane, c), :] = value[c * YL : (c + 1) * YL, :]

    def pull(plane):
        fields[place(plane, 3), :] = unstacked("pull parts", plane)[0:YL, :]

    def second_delta(plane):
        d2.put(plane, dot(t3_ref[...], sg.window(plane)) * slope2[plane])

    def first_delta(plane):
        d1.put(plane, dot(t2_ref[...], d2.window(plane)) * slope1[plane])

    def add_product(name, delta, count, source, plane):
        term = product(delta, count, source, plane)
        sums[name] = sums[name] + term if name in sums else term

    def bind(step, *given):
        return functools.partial(step, *given)

    for slab in range(slabs):
        plan.add("load", slab, [], bind(load, slab))
    for p in range(depth):
        slabs_near = [("load", q // ZL) for _, q in near("", p)]
        plan.add("first", p, slabs_near, bind(first_layer, p))
    for p in range(depth):
        plan.add("second", p, near("first", p), bind(second_layer, p))
    for p in range(depth):
        plan.add("force parts", p, [("second", p)], bind(stacked, "force parts", b3_ref, s2, p))
    for p in range(depth):
        plan.add("force", p, near("force parts", p), bind(force, p))
    groups = range(0, depth, 4)
    for p in groups:
        after = [("second", q % depth) for q in range(p - 1, p + 5)]
        plan.add("last sum", p, after, bind(add_product, "last", sg, 3 * POS, s2, p))
    for p in range(depth):
        plan.add("second delta", p, [("second", p)], bind(second_delta, p))
    for p in groups:
        after = [("second delta", q) for q in range(p, p + 4)]
        plan.add("middle sum", p, after, bind(add_product, "middle", d2, YL * channels, s1, p))
    for p in range(depth):
        plan.add("first delta", p, near("second delta", p), bind(first_delta, p))
    for p in groups:
        after = [("first delta", q) for q in range(p, p + 4)]
        plan.add("first sum", p, after, bind(add_product, "first", d1, YL * channels, s0, p))
    for p in range(depth):
        plan.add("pull parts", p, [("first delta", p)], bind(stacked, "pull parts", t1_ref, d1, p))
    for p in range(depth):
        plan.add("pull", p, near("pull parts", p), bind(pull, p))
    plan.in_turn()
    mesh_ref[...] = fields[...].astype(BF16)
    for first, name, table_ref, ins, mixed in (
        (0, "first", c1_ref, 1, True),
        (8, "middle", c2_ref, channels, True),
        (16, "last", c3_ref, channels, False),
    ):
        outs = channels if mixed else 3
        grads_ref[first : first + 8, 0 : 27 * ins] = weight_sum(
            sums[name], table_ref[...], ins, mixed, outs
        )


def network(halves, band_list, channels, slabs):
    depth = slabs * ZL
    order = np.zeros((64, 64), np.float32)
    for z in range(4):
        for y in range(4):
            for h, place in enumerate((y, 4 + y, 8 + 2 * y, 15 - 2 * y)):
                order[z * 16 + place, h * 16 + z * 4 + y] = 1.0
    planes = 3 * (depth + 2)
    shared = slabs > 4
    sizes = [POS, 3 * POS, 14 * channels, (12 if shared else 10) * channels]
    stores = [pltpu.VMEM((planes * n, XL), BF16) for n in sizes]
    more = [] if shared else [12 * channels, 10 * channels]
    slopes = [pltpu.VMEM((depth, n * channels, XL), F32) for n in (10, 12)]
    size = sum(sizes + more) * planes * XL * 2 + (22 * channels + 32) * depth * XL * 4
    tables = [jnp.asarray(t) for t in (window_columns(16, 1), window_columns(14, channels), window_columns(10, channels))]
    given = (*halves, *band_list, jnp.asarray(order, BF16), *tables)
    return pl.pallas_call(
        functools.partial(net_kernel, slabs, channels, shared),
        in_specs=[VMEM] * len(given),
        out_specs=[VMEM] * 2,
        out_shape=[
            jax.ShapeDtypeStruct((slabs * FIELDS * ROWS, XL), BF16),
            jax.ShapeDtypeStruct((24, 256), F32),
        ],
        scratch_shapes=stores
        + slopes
        + [pltpu.VMEM((slabs * FIELDS * ROWS, XL), F32)]
        + [pltpu.VMEM((planes * n, XL), BF16) for n in more],
        compiler_params=limit(size + 12 * MIB),
    )(*given)


def readout_kernel(slabs, chunk, step_ref, slab_ref, cell_ref, velocity_ref, mesh_ref, *rest):
    velocity_out, mass_out, lane_hot, mass_rows = rest
    cell = cell_ref[...]
    code = slab_ref[...] * ROWS + (cell >> 8)
    lanes = (cell & (XL - 1)).astype(F32)
    eight = row_iota((8, chunk), 0)
    tiles = chunk // 128
    height = FIELDS * ROWS
    for turn in range(cell.shape[0] // tiles):
        here = lane_hot.at[turn % 2]
        fill_lane_hot(here, spread_rows(lanes, 16, turn * tiles, tiles).astype(BF16), chunk)
        code_tile = spread_rows(code, 8, turn * tiles, tiles)
        sums = [jnp.zeros((8, chunk), F32) for _ in range(FIELDS)]
        everything = dot(mesh_ref[...], here[...])
        for k in range(slabs):
            rows = everything[k * height : (k + 1) * height, :]
            for group in range(ROWS // 8):
                same = code_tile == eight + (k * ROWS + group * 8)
                for c in range(FIELDS):
                    first = c * ROWS + group * 8
                    sums[c] = sums[c] + jnp.where(same, rows[first : first + 8, :], 0.0)
        span = slice(turn * chunk, (turn + 1) * chunk)
        for c in range(3):
            force = jnp.sum(sums[c], axis=0, keepdims=True)
            velocity_out[c : c + 1, span] = velocity_ref[c : c + 1, span] + step_ref[0] * force
        pull = jnp.sum(sums[3], axis=0, keepdims=True)
        for t in range(tiles):
            mass_rows[turn * tiles + t : turn * tiles + t + 1, :] = pull[:, t * 128 : (t + 1) * 128]
    mass_out[...] = mass_rows[...].astype(BF16)


def read_out(step_size, target, cells, velocity, mesh, slabs):
    count = velocity.shape[1]
    chunk = math.gcd(count, 1024)
    return pl.pallas_call(
        functools.partial(readout_kernel, slabs, chunk),
        in_specs=[SMEM] + [VMEM] * 4,
        out_specs=[VMEM] * 2,
        out_shape=[
            jax.ShapeDtypeStruct((3, count), F32),
            jax.ShapeDtypeStruct((count // 128, 128), BF16),
        ],
        scratch_shapes=[
            pltpu.VMEM((2, XL, chunk), BF16),
            pltpu.VMEM((count // 128, 128), F32),
        ],
        compiler_params=limit((16 + 4 * slabs) * MIB),
        cost_estimate=pl.CostEstimate(
            flops=slabs * 2 * FIELDS * ROWS * XL * count, bytes_accessed=1_000_000, transcendentals=0
        ),
    )(step_size, target, cells, velocity, mesh)


def total_kernel(scale, *refs):
    grads, outs = refs[:-3], refs[-3:]
    total = grads[0][...]
    for other in grads[1:]:
        total = total + other[...]
    total = total * scale
    for first, out in zip((0, 8, 16), outs):
        out[...] = total[first : first + out.shape[0], 0 : out.shape[1]]


def add_up(grads, weights, scale):
    return pl.pallas_call(
        functools.partial(total_kernel, scale),
        in_specs=[VMEM] * len(grads),
        out_specs=[VMEM] * 3,
        out_shape=[jax.ShapeDtypeStruct(w.shape, F32) for w in weights],
        compiler_params=limit(4 * MIB),
    )(*grads)


def shifted(value, axis, distance):
    count = lax.axis_size(axis)
    return lax.ppermute(value, axis, [(i, (i + distance) % count) for i in range(count)])


def from_all(value, axis):
    count = lax.axis_size(axis)
    values = value if isinstance(value, (list, tuple)) else [value] * count
    others = []
    order = list(range(1, count))
    if count > 3:
        order = order[1:2] + order[0:1] + order[2:]
    for n, k in enumerate(order, 1):
        if count & (count - 1):
            others.append(shifted(values[n], axis, -k))
        else:
            others.append(lax.ppermute(values[n], axis, [(i, i ^ k) for i in range(count)]))
    return [values[0]] + others


def local(masses, velocity, dest_slab, dest_cell, w_first, w_middle, w_last, step_size, cotangent):
    slabs = lax.axis_size("slab")
    column = ("pencil", "sub")
    count = masses.shape[0]
    dense = (count // 128, 128)
    target, cells = dest_slab.reshape(dense), dest_cell.reshape(dense)
    packed = pack(step_size, masses.reshape(dense), target, cells, cotangent, slabs)
    messages = from_all(packed, "slab")
    painted = None
    for message in messages[:-1]:
        painted = paint(painted, [message], dense[0], slabs)
    high = paint(painted, messages[-1:], dense[0], slabs, 1)
    before = shifted(high, column, 1)
    low = paint(painted, messages[-1:], dense[0], slabs, 0)
    low, w_first, w_middle, w_last = lax.optimization_barrier((low, w_first, w_middle, w_last))
    after = shifted(low, column, -1)
    band_list = bands(w_first, w_middle, w_last)
    mesh, grads = network((low, high, after, before), band_list, w_middle.shape[0], slabs)
    all_grads = from_all(grads, column)
    velocity_new, grad_mass = read_out(step_size, target, cells, velocity, mesh, slabs)
    cell_total = ZL * YL * XL * slabs * lax.axis_size("pencil") * lax.axis_size("sub")
    weight_grads = add_up(all_grads, (w_first, w_middle, w_last), 1.0 / math.sqrt(cell_total))
    return (velocity_new, grad_mass.reshape(count), *weight_grads)


def solution(mesh):
    everywhere = ("runs", "slab", "pencil", "sub")
    placed = (
        P(everywhere),
        P(None, everywhere),
        P(everywhere, None),
        P(everywhere),
        P(),
        P(),
        P(),
        P(),
        P(None, everywhere),
    )
    return jax.shard_map(
        local,
        mesh=mesh,
        in_specs=placed,
        out_specs=(
            P(None, everywhere),
            P(everywhere),
            P("runs", None),
            P("runs", None),
            P("runs", None),
        ),
        check_vma=False,
    )
```

```python
import functools
import math

import jax
import jax.numpy as jnp
import numpy as np
from jax import lax
from jax.experimental import pallas as pl
from jax.experimental.pallas import tpu as pltpu
from jax.sharding import PartitionSpec as P

ZL = 4
YL = 8
XL = 256
ROWS = ZL * YL
FIELDS = 4
POS = 16
HALF = POS // 4
BF16 = jnp.bfloat16
F32 = jnp.float32
NT = (((1,), (1,)), ((), ()))
MIB = 1024 * 1024
VMEM = pl.BlockSpec(memory_space=pltpu.VMEM)
SMEM = pl.BlockSpec(memory_space=pltpu.SMEM)


def dot(a, b):
    return jnp.dot(a, b, preferred_element_type=F32)


def dot_nt(a, b):
    return lax.dot_general(a, b, NT, preferred_element_type=F32)


def row_iota(shape, dim):
    return lax.broadcasted_iota(jnp.int32, shape, dim)


def limit(size):
    return pltpu.CompilerParams(vmem_limit_bytes=size)


def pack_kernel(step_ref, mass_ref, slab_ref, cell_ref, cot_ref, *rest):
    outs, rows = rest[:-1], rest[-1]
    tiles = mass_ref.shape[0]
    cell, slab = cell_ref[...], slab_ref[...]
    z, y = cell >> 11, (cell >> 8) & 7
    code = ((slab & 7) << 5) + ((y >> 2) << 4) + (z << 2) + (y & 3)
    for component in range(3):
        for t in range(tiles):
            row = component * tiles + t
            rows[row : row + 1, :] = cot_ref[component : component + 1, t * 128 : (t + 1) * 128]
    parts = [mass_ref[...], (step_ref[0] * rows[...]).astype(BF16)]
    lane = cell & (XL - 1)
    if outs[0].shape[0] == 5 * tiles:
        value = (128 + (lane & 127)).astype(F32) * jnp.exp2((code - 64).astype(F32))
        parts.append(jnp.where(lane > 127, -value, value).astype(BF16))
    else:
        parts += [part.astype(F32).astype(BF16) for part in (code, lane, slab >> 3)]
    for out_ref in outs:
        first = 0
        for part in parts:
            if first < out_ref.shape[0]:
                out_ref[first : first + part.shape[0], :] = part
            first += part.shape[0]


def message_rows(slabs):
    return 5 if slabs <= 4 else 6 if slabs <= 8 else 7


def pack(step_size, masses, target, cells, cotangent, slabs):
    tiles = masses.shape[0]
    shape = jax.ShapeDtypeStruct((message_rows(slabs) * tiles, 128), BF16)
    return pl.pallas_call(
        pack_kernel,
        in_specs=[SMEM] + [VMEM] * 4,
        out_specs=[VMEM] * slabs,
        out_shape=[shape] * slabs,
        scratch_shapes=[pltpu.VMEM((3 * tiles, 128), F32)],
        compiler_params=limit(60 * MIB),
    )(step_size, masses, target, cells, cotangent)


def spread_rows(dense, height, first, count):
    tiles = [
        jnp.broadcast_to(dense[t : t + 1, :], (height, 128)) for t in range(first, first + count)
    ]
    return jnp.concatenate(tiles, axis=1)


def fill_lane_hot(store, lane, chunk):
    sixteen = row_iota((16, chunk), 0)
    zero, one = jnp.zeros((16, chunk), BF16), jnp.ones((16, chunk), BF16)
    for group in range(XL // 16):
        same = lane == (sixteen + 16 * group).astype(F32).astype(BF16)
        store[16 * group : 16 * group + 16, :] = jnp.where(same, one, zero)


def cell_parts(message, tiles, slabs):
    value = message[4 * tiles : 5 * tiles, :].astype(F32)
    if message_rows(slabs) > 5:
        return value, message[5 * tiles : 6 * tiles, :].astype(F32)
    size = jnp.abs(value)
    power = jnp.floor(jnp.log2(size) + 0.002)
    mantissa = jnp.floor(size * jnp.exp2(-power) * 128.0 + 0.5)
    return power + 57.0, jnp.where(value < 0.0, mantissa, mantissa - 128.0)


def paint_kernel(slabs, chunk, tiles, started, halves, count, *refs):
    before, refs = (refs[0], refs[1:]) if started else (None, refs)
    messages, refs = refs[:count], refs[count:]
    outs, (hot, lane_hot, total) = refs[:-3], refs[-3:]
    step = chunk // 128
    sixteen = row_iota((16, chunk), 0)
    zero = jnp.zeros((16, chunk), BF16)
    for number in range(count * (tiles // step)):
        message, turn = messages[number // (tiles // step)], number % (tiles // step)
        here, here_lane = hot.at[turn % 2], lane_hot.at[turn % 2]

        def spread(field):
            rows = message[field * tiles : (field + 1) * tiles, :].astype(F32)
            return spread_rows(rows, 16, turn * step, step)

        if turn == 0:
            codes, lanes = cell_parts(message, tiles, slabs)
        lane = spread_rows(lanes, 16, turn * step, step).astype(BF16)
        fill_lane_hot(here_lane, lane, chunk)
        values = [spread(field).astype(BF16) for field in range(FIELDS)]
        code = spread_rows(codes, 16, turn * step, step)
        for eight in range(0, slabs, 8):
            code_tile = code if slabs <= 8 else jnp.where(spread(6) == eight // 8, code, -1.0)
            code_tile = code_tile.astype(BF16)
            for slab in range(eight, min(eight + 8, slabs)):
                for number_of, half in enumerate(halves):
                    place = ((slab - eight) * 2 + half) * 16
                    same = code_tile == (sixteen + place).astype(F32).astype(BF16)
                    for field in range(FIELDS):
                        first = ((number_of * FIELDS + field) * slabs + slab) * 16
                        here[first : first + 16, :] = jnp.where(same, values[field], zero)
        part = dot_nt(here[...], here_lane[...])
        if number > 0:
            total[...] += part
        elif started:
            skip = before.shape[0] - total.shape[0] if halves[0] else 0
            total[...] = before[skip : skip + total.shape[0], :] + part
        else:
            total[...] = part
    outs[0][...] = total[...].astype(outs[0].dtype)


def paint(before, messages, tiles, slabs, half=None):
    chunk = 128 * math.gcd(tiles, 16)
    halves = (0, 1) if half is None else (half,)
    height = len(halves) * FIELDS * slabs * 16
    scratch = 2 * chunk * (height + XL) * 2 + height * XL * 4
    shapes = [jax.ShapeDtypeStruct((height, XL), F32 if half is None else BF16)]
    given = messages if before is None else [before] + messages
    return pl.pallas_call(
        functools.partial(
            paint_kernel, slabs, chunk, tiles, before is not None, halves, len(messages)
        ),
        in_specs=[VMEM] * len(given),
        out_specs=[VMEM] * len(shapes),
        out_shape=shapes,
        scratch_shapes=[
            pltpu.VMEM((2, height, chunk), BF16),
            pltpu.VMEM((2, XL, chunk), BF16),
            pltpu.VMEM((height, XL), F32),
        ],
        compiler_params=limit(scratch + height * XL * 24 + 12 * MIB),
        cost_estimate=pl.CostEstimate(
            flops=2 * height * XL * tiles * 128 * len(messages), bytes_accessed=MIB, transcendentals=0
        ),
    )(*given)[0]


def y_of(place):
    rest = place - 8
    if isinstance(place, np.ndarray):
        return np.where(place < 8, place + 4, np.where(rest % 2 == 0, 12 + rest // 2, 3 - rest // 2))
    halo = jnp.where((rest & 1) == 0, 12 + (rest >> 1), 3 - (rest >> 1))
    return jnp.where(place < 8, place + 4, halo)


def columns(rows, channels):
    col = np.arange(9 * rows * channels)
    pair, place, channel = col // (rows * channels), col // channels % rows, col % channels
    taps = [((pair // 3 * 3 + b) * 3 + pair % 3) * channels + channel for b in range(3)]
    return np.stack(taps + [y_of(place)] + [np.zeros_like(col)] * 4).astype(np.int32)


def window_columns(rows, channels):
    col = np.arange(3 * rows * channels)
    listed = [y_of(col // channels % rows), col // (rows * channels) * channels + col % channels]
    return np.stack(listed + [np.zeros_like(col)] * 6).astype(np.int32)


def band(weight, table, row_channel, row_place):
    outs, count = weight.shape
    width = table.shape[1]
    rows = row_channel.shape[0]
    pick = jnp.where(row_channel[:, 0:outs] == row_iota((rows, outs), 1), 1.0, 0.0)
    spread = dot(pick.astype(BF16), weight).astype(BF16)
    distance = table[3:4, :] - y_of(row_place)
    result = jnp.zeros((rows, width), F32)
    for b in range(3):
        same = row_iota((count, width), 0) == table[b : b + 1, :]
        picked = dot(spread, jnp.where(same, 1.0, 0.0).astype(BF16))
        result = jnp.where(distance == b - 1, picked, result)
    return result


def band_kernel(
    first_ref, middle_ref, last_ref, c1_ref, c2_ref, c3_ref,
    b1_ref, b2_ref, b3_ref, t1_ref, t2_ref, t3_ref,
):
    channels = first_ref.shape[0]
    bits = channels.bit_length() - 1

    def mixed(rows, width):
        row = row_iota((rows, width), 0)
        return row & (channels - 1), row >> bits

    def turned(full, pair, width, rows, out_ref):
        block = full[:, pair * width : (pair + 1) * width].T[0:rows].astype(BF16)
        out_ref[:, (8 - pair) * block.shape[1] : (9 - pair) * block.shape[1]] = block

    def stack(out_ref, pair, block):
        rows, width = block.shape
        first = pair % 3 * width
        out_ref[pair // 3 * rows : (pair // 3 + 1) * rows, first : first + width] = block

    rows = b1_ref.shape[0]
    table = c1_ref[...]
    full = band(first_ref[...], table, mixed(rows, 128)[0], mixed(rows, table.shape[1])[1])
    b1_ref[...] = full.astype(BF16)
    short = t1_ref.shape[1] // 3
    for pair in range(9):
        stack(t1_ref, 8 - pair, full[0:short, pair * POS : (pair + 1) * POS].T.astype(BF16))
    rows = b2_ref.shape[0]
    table = c2_ref[...]
    full = band(middle_ref[...], table, mixed(rows, 128)[0], mixed(rows, table.shape[1])[1])
    b2_ref[...] = full.astype(BF16)
    for pair in range(9):
        turned(full, pair, full.shape[1] // 9, t2_ref.shape[0], t2_ref)
    rows = 3 * POS
    table = c3_ref[...]
    channel = row_iota((rows, 128), 0) >> 4
    full = band(last_ref[...], table, channel, row_iota((rows, table.shape[1]), 0) & (POS - 1))
    width, short = full.shape[1] // 9, b3_ref.shape[1] // 3
    own = [full[o * POS : o * POS + YL] for o in range(3)] + [jnp.zeros((YL, full.shape[1]), F32)]
    own = jnp.concatenate(own, axis=0).astype(BF16)
    for pair in range(9):
        stack(b3_ref, pair, own[:, pair * width : pair * width + short])
        turned(full, pair, width, t3_ref.shape[0], t3_ref)


def bands(w_first, w_middle, w_last):
    c = w_middle.shape[0]
    tables = [jnp.asarray(t) for t in (columns(16, 1), columns(14, c), columns(12, c))]
    shapes = [
        (14 * c, 9 * 16), (12 * c, 9 * 14 * c), (3 * 4 * YL, 3 * 10 * c),
        (3 * POS, 3 * 10 * c), (10 * c, 9 * 12 * c), (12 * c, 9 * 3 * POS),
    ]
    return pl.pallas_call(
        band_kernel,
        in_specs=[VMEM] * 6,
        out_specs=[VMEM] * 6,
        out_shape=[jax.ShapeDtypeStruct(s, BF16) for s in shapes],
        compiler_params=limit(20 * MIB),
        cost_estimate=pl.CostEstimate(
            flops=800_000_000, bytes_accessed=4_000_000, transcendentals=0
        ),
    )(w_first, w_middle, w_last, *tables)


def slope(pre, sigma):
    return sigma * (1.0 + pre * (1.0 - sigma))


def split_three(value):
    high = value.astype(BF16).astype(F32)
    rest = value - high
    mid = rest.astype(BF16).astype(F32)
    return jnp.concatenate([high, mid, rest - mid], axis=0).astype(BF16)


def weight_sum(full, table, channels, mixed, outs):
    count, width = full.shape[0] // 3, full.shape[1]
    group = row_iota((3 * channels, width), 0) == table[1:2, :]
    group = jnp.where(group, 1.0, 0.0).astype(BF16)
    picked = []
    for b in range(3):
        for e in range(3):
            block = full[e * count : (e + 1) * count, :]
            if mixed:
                parts = [
                    jnp.where(table[0:1, :] == place + 3 + b, block[place * 8 : place * 8 + 8, :], 0.0)
                    for place in range(YL)
                ]
                picked.append(functools.reduce(jnp.add, parts))
                continue
            wanted = table[0:1, :] - row_iota((YL, width), 0) == 3 + b
            rows = [
                jnp.sum(
                    jnp.where(wanted, block[o * POS : o * POS + YL, :], 0.0), axis=0, keepdims=True
                )
                for o in range(outs)
            ]
            picked.append(jnp.concatenate(rows + [jnp.zeros_like(rows[0])] * (8 - outs), axis=0))
    parts = dot_nt(split_three(jnp.concatenate(picked, axis=0)), group)
    total = parts[0:72] + parts[72:144] + parts[144:216]
    pieces = [
        total[pair * 8 : pair * 8 + 8, a * channels : (a + 1) * channels]
        for a in range(3)
        for pair in range(9)
    ]
    return jnp.concatenate(pieces, axis=1)


class Store:
    def __init__(self, ref, depth, rows):
        self.ref, self.depth, self.rows = ref, depth, rows

    def put(self, plane, value, first=0):
        places = [plane + 1]
        if plane == 0:
            places.append(self.depth + 1)
        if plane == self.depth - 1:
            places.append(0)
        for e, shift in enumerate((1, 0, XL - 1)):
            moved = (value if shift == 0 else pltpu.roll(value, shift, 1)).astype(BF16)
            for place in places:
                row = (place * 3 + e) * self.rows + first
                self.ref[row : row + value.shape[0], :] = moved

    def window(self, plane):
        return self.ref[plane * 3 * self.rows : (plane + 3) * 3 * self.rows, :]

    def plane(self, plane):
        return self.ref[(plane + 1) * 3 * self.rows : (plane + 2) * 3 * self.rows, :]

    def shifted(self, plane, e, count):
        row = ((plane + 1) * 3 + e) * self.rows
        return self.ref[row : row + count, :]


def product(delta, count, source, plane):
    planes = range(plane, plane + 4)
    left = [
        jnp.concatenate([delta.shifted(p, e, count) for e in (2, 1, 0)], axis=0) for p in planes
    ]
    right = [
        jnp.concatenate([source.shifted(p + a, 1, source.rows) for a in (-1, 0, 1)], axis=0)
        for p in planes
    ]
    return dot_nt(jnp.concatenate(left, axis=1), jnp.concatenate(right, axis=1))


class Plan:
    def __init__(self):
        self.stages = {}

    def add(self, stage, key, after, step):
        self.stages.setdefault(stage, []).append((key, after, step))

    def in_turn(self):
        for steps in self.stages.values():
            for _, _, step in steps:
                step()


def net_kernel(
    slabs, channels, shared,
    low_ref, high_ref, after_ref, before_ref,
    b1_ref, b2_ref, b3_ref, t1_ref, t2_ref, t3_ref, order_ref, c1_ref, c2_ref, c3_ref,
    mesh_ref, grads_ref,
    s0_ref, sg_ref, a_ref, b_ref, slope1, slope2, fields, *more,
):
    depth = slabs * ZL
    s0, sg = Store(s0_ref, depth, POS), Store(sg_ref, depth, 3 * POS)
    s1, s2 = Store(a_ref, depth, 14 * channels), Store(b_ref, depth, 10 * channels)
    d2 = Store(b_ref if shared else more[0], depth, 12 * channels)
    d1 = Store(a_ref if shared else more[1], depth, 10 * channels)
    order = order_ref[...]
    grads_ref[...] = jnp.zeros_like(grads_ref)
    inner = 10 * channels
    plan, kept, sums = Plan(), {}, {}

    def near(stage, plane):
        return [(stage, (plane + a) % depth) for a in (-1, 0, 1)]

    def place(plane, field):
        first = (plane // ZL * FIELDS + field) * ROWS + plane % ZL * YL
        return slice(first, first + YL)

    def load(slab):
        for c in range(FIELDS):
            first = (c * slabs + slab) * 16
            pieces = [ref[first : first + 16, :] for ref in (low_ref, high_ref, after_ref, before_ref)]
            rows = dot(order, jnp.concatenate(pieces, axis=0))
            for z in range(ZL):
                value = rows[z * POS : (z + 1) * POS, :]
                if c == 0:
                    s0.put(slab * ZL + z, value)
                else:
                    sg.put(slab * ZL + z, value, (c - 1) * POS)

    def first_layer(plane):
        pre = dot(b1_ref[...], s0.window(plane))
        sigma = jax.nn.sigmoid(pre)
        s1.put(plane, pre * sigma)
        slope1[plane] = slope(pre[0:inner], sigma[0:inner])

    def second_layer(plane):
        pre = dot(b2_ref[...], s1.window(plane))
        sigma = jax.nn.sigmoid(pre)
        s2.put(plane, pre[0:inner] * sigma[0:inner])
        slope2[plane] = slope(pre, sigma)

    def stacked(stage, weight_ref, store, plane):
        kept[stage, plane] = dot(weight_ref[...], store.plane(plane))

    def unstacked(stage, plane):
        rows = kept[stage, plane].shape[0] // 3
        return functools.reduce(
            jnp.add,
            [kept[key][a * rows : (a + 1) * rows] for a, key in enumerate(near(stage, plane))],
        )

    def force(plane):
        value = unstacked("force parts", plane)
        for c in range(3):
            fields[place(plane, c), :] = value[c * YL : (c + 1) * YL, :]

    def pull(plane):
        fields[place(plane, 3), :] = unstacked("pull parts", plane)[0:YL, :]

    def second_delta(plane):
        d2.put(plane, dot(t3_ref[...], sg.window(plane)) * slope2[plane])

    def first_delta(plane):
        d1.put(plane, dot(t2_ref[...], d2.window(plane)) * slope1[plane])

    def add_product(name, delta, count, source, plane):
        term = product(delta, count, source, plane)
        sums[name] = sums[name] + term if name in sums else term

    def bind(step, *given):
        return functools.partial(step, *given)

    for slab in range(slabs):
        plan.add("load", slab, [], bind(load, slab))
    for p in range(depth):
        slabs_near = [("load", q // ZL) for _, q in near("", p)]
        plan.add("first", p, slabs_near, bind(first_layer, p))
    for p in range(depth):
        plan.add("second", p, near("first", p), bind(second_layer, p))
    for p in range(depth):
        plan.add("force parts", p, [("second", p)], bind(stacked, "force parts", b3_ref, s2, p))
    for p in range(depth):
        plan.add("force", p, near("force parts", p), bind(force, p))
    groups = range(0, depth, 4)
    for p in groups:
        after = [("second", q % depth) for q in range(p - 1, p + 5)]
        plan.add("last sum", p, after, bind(add_product, "last", sg, 3 * POS, s2, p))
    for p in range(depth):
        plan.add("second delta", p, [("second", p)], bind(second_delta, p))
    for p in groups:
        after = [("second delta", q) for q in range(p, p + 4)]
        plan.add("middle sum", p, after, bind(add_product, "middle", d2, YL * channels, s1, p))
    for p in range(depth):
        plan.add("first delta", p, near("second delta", p), bind(first_delta, p))
    for p in groups:
        after = [("first delta", q) for q in range(p, p + 4)]
        plan.add("first sum", p, after, bind(add_product, "first", d1, YL * channels, s0, p))
    for p in range(depth):
        plan.add("pull parts", p, [("first delta", p)], bind(stacked, "pull parts", t1_ref, d1, p))
    for p in range(depth):
        plan.add("pull", p, near("pull parts", p), bind(pull, p))
    plan.in_turn()
    mesh_ref[...] = fields[...].astype(BF16)
    for first, name, table_ref, ins, mixed in (
        (0, "first", c1_ref, 1, True),
        (8, "middle", c2_ref, channels, True),
        (16, "last", c3_ref, channels, False),
    ):
        outs = channels if mixed else 3
        grads_ref[first : first + 8, 0 : 27 * ins] = weight_sum(
            sums[name], table_ref[...], ins, mixed, outs
        )


def network(halves, band_list, channels, slabs):
    depth = slabs * ZL
    order = np.zeros((64, 64), np.float32)
    for z in range(4):
        for y in range(4):
            for h, place in enumerate((y, 4 + y, 8 + 2 * y, 15 - 2 * y)):
                order[z * 16 + place, h * 16 + z * 4 + y] = 1.0
    planes = 3 * (depth + 2)
    shared = slabs > 4
    sizes = [POS, 3 * POS, 14 * channels, (12 if shared else 10) * channels]
    stores = [pltpu.VMEM((planes * n, XL), BF16) for n in sizes]
    more = [] if shared else [12 * channels, 10 * channels]
    slopes = [pltpu.VMEM((depth, n * channels, XL), F32) for n in (10, 12)]
    size = sum(sizes + more) * planes * XL * 2 + (22 * channels + 32) * depth * XL * 4
    tables = [jnp.asarray(t) for t in (window_columns(16, 1), window_columns(14, channels), window_columns(10, channels))]
    given = (*halves, *band_list, jnp.asarray(order, BF16), *tables)
    return pl.pallas_call(
        functools.partial(net_kernel, slabs, channels, shared),
        in_specs=[VMEM] * len(given),
        out_specs=[VMEM] * 2,
        out_shape=[
            jax.ShapeDtypeStruct((slabs * FIELDS * ROWS, XL), BF16),
            jax.ShapeDtypeStruct((24, 256), F32),
        ],
        scratch_shapes=stores
        + slopes
        + [pltpu.VMEM((slabs * FIELDS * ROWS, XL), F32)]
        + [pltpu.VMEM((planes * n, XL), BF16) for n in more],
        compiler_params=limit(size + 12 * MIB),
    )(*given)


def readout_kernel(slabs, chunk, step_ref, slab_ref, cell_ref, velocity_ref, mesh_ref, *rest):
    velocity_out, mass_out, lane_hot, mass_rows = rest
    cell = cell_ref[...]
    code = slab_ref[...] * ROWS + (cell >> 8)
    lanes = (cell & (XL - 1)).astype(F32)
    eight = row_iota((8, chunk), 0)
    tiles = chunk // 128
    height = FIELDS * ROWS
    for turn in range(cell.shape[0] // tiles):
        here = lane_hot.at[turn % 2]
        fill_lane_hot(here, spread_rows(lanes, 16, turn * tiles, tiles).astype(BF16), chunk)
        code_tile = spread_rows(code, 8, turn * tiles, tiles)
        sums = [jnp.zeros((8, chunk), F32) for _ in range(FIELDS)]
        everything = dot(mesh_ref[...], here[...])
        for k in range(slabs):
            rows = everything[k * height : (k + 1) * height, :]
            for group in range(ROWS // 8):
                same = code_tile == eight + (k * ROWS + group * 8)
                for c in range(FIELDS):
                    first = c * ROWS + group * 8
                    sums[c] = sums[c] + jnp.where(same, rows[first : first + 8, :], 0.0)
        span = slice(turn * chunk, (turn + 1) * chunk)
        for c in range(3):
            force = jnp.sum(sums[c], axis=0, keepdims=True)
            velocity_out[c : c + 1, span] = velocity_ref[c : c + 1, span] + step_ref[0] * force
        pull = jnp.sum(sums[3], axis=0, keepdims=True)
        for t in range(tiles):
            mass_rows[turn * tiles + t : turn * tiles + t + 1, :] = pull[:, t * 128 : (t + 1) * 128]
    mass_out[...] = mass_rows[...].astype(BF16)


def read_out(step_size, target, cells, velocity, mesh, slabs):
    count = velocity.shape[1]
    chunk = math.gcd(count, 1024)
    return pl.pallas_call(
        functools.partial(readout_kernel, slabs, chunk),
        in_specs=[SMEM] + [VMEM] * 4,
        out_specs=[VMEM] * 2,
        out_shape=[
            jax.ShapeDtypeStruct((3, count), F32),
            jax.ShapeDtypeStruct((count // 128, 128), BF16),
        ],
        scratch_shapes=[
            pltpu.VMEM((2, XL, chunk), BF16),
            pltpu.VMEM((count // 128, 128), F32),
        ],
        compiler_params=limit((16 + 4 * slabs) * MIB),
        cost_estimate=pl.CostEstimate(
            flops=slabs * 2 * FIELDS * ROWS * XL * count, bytes_accessed=1_000_000, transcendentals=0
        ),
    )(step_size, target, cells, velocity, mesh)


def total_kernel(scale, *refs):
    grads, outs = refs[:-3], refs[-3:]
    total = grads[0][...]
    for other in grads[1:]:
        total = total + other[...]
    total = total * scale
    for first, out in zip((0, 8, 16), outs):
        out[...] = total[first : first + out.shape[0], 0 : out.shape[1]]


def add_up(grads, weights, scale):
    return pl.pallas_call(
        functools.partial(total_kernel, scale),
        in_specs=[VMEM] * len(grads),
        out_specs=[VMEM] * 3,
        out_shape=[jax.ShapeDtypeStruct(w.shape, F32) for w in weights],
        compiler_params=limit(4 * MIB),
    )(*grads)


def shifted(value, axis, distance):
    count = lax.axis_size(axis)
    return lax.ppermute(value, axis, [(i, (i + distance) % count) for i in range(count)])


def from_all(value, axis):
    count = lax.axis_size(axis)
    values = value if isinstance(value, (list, tuple)) else [value] * count
    others = []
    order = list(range(1, count))
    if count > 3:
        order = order[1:2] + order[0:1] + order[2:]
    for n, k in enumerate(order, 1):
        if count & (count - 1):
            others.append(shifted(values[n], axis, -k))
        else:
            others.append(lax.ppermute(values[n], axis, [(i, i ^ k) for i in range(count)]))
    return [values[0]] + others


def local(masses, velocity, dest_slab, dest_cell, w_first, w_middle, w_last, step_size, cotangent):
    slabs = lax.axis_size("slab")
    column = ("pencil", "sub")
    count = masses.shape[0]
    dense = (count // 128, 128)
    target, cells = dest_slab.reshape(dense), dest_cell.reshape(dense)
    packed = pack(step_size, masses.reshape(dense), target, cells, cotangent, slabs)
    messages = from_all(packed, "slab")
    painted = None
    for message in messages[:-1]:
        painted = paint(painted, [message], dense[0], slabs)
    high = paint(painted, messages[-1:], dense[0], slabs, 1)
    before = shifted(high, column, 1)
    low = paint(painted, messages[-1:], dense[0], slabs, 0)
    low, w_first, w_middle, w_last = lax.optimization_barrier((low, w_first, w_middle, w_last))
    after = shifted(low, column, -1)
    band_list = bands(w_first, w_middle, w_last)
    mesh, grads = network((low, high, after, before), band_list, w_middle.shape[0], slabs)
    all_grads = from_all(grads, column)
    velocity_new, grad_mass = read_out(step_size, target, cells, velocity, mesh, slabs)
    cell_total = ZL * YL * XL * slabs * lax.axis_size("pencil") * lax.axis_size("sub")
    weight_grads = add_up(all_grads, (w_first, w_middle, w_last), 1.0 / math.sqrt(cell_total))
    return (velocity_new, grad_mass.reshape(count), *weight_grads)


def solution(mesh):
    everywhere = ("runs", "slab", "pencil", "sub")
    placed = (
        P(everywhere),
        P(None, everywhere),
        P(everywhere, None),
        P(everywhere),
        P(),
        P(),
        P(),
        P(),
        P(None, everywhere),
    )
    return jax.shard_map(
        local,
        mesh=mesh,
        in_specs=placed,
        out_specs=(
            P(None, everywhere),
            P(everywhere),
            P("runs", None),
            P("runs", None),
            P("runs", None),
        ),
        check_vma=False,
    )
```
